512 devices in a mesh: video: 8 (over y, core), tm: 64 (over x, z).
Axes of the slice: x: 4, y: 4, z: 16, core: 2. Of those that a mesh axis runs over, the one named last changes fastest.
Arguments:
- tokens: bfloat16 [131072, 1152], P(('video', 'tm')), parts along dimension 0, may hold values from -1000 to 1000
- gain: bfloat16 [1152], replicated, may hold values from 0.099609375 to 1.8984375
- w_query: bfloat16 [1152, 640], P('tm'), may hold values from -0.5 to 0.5
- w_key: bfloat16 [1152, 640], P('tm'), may hold values from -0.5 to 0.5
- w_value: bfloat16 [1152, 640], P('tm'), may hold values from -0.1875 to 0.1875
- conv_weight: bfloat16 [27, 640], replicated, may hold values from -1.25 to 1.25
Outputs:
- mixed: float32 [131072, 640], P(('video', 'tm')), parts along dimension 0
The draws below stay inside these ranges and needn't reach their ends.
There are 8 independent parts, one for each index of `video`. The reference program is written for one: setup_inputs(seed, part) draws one part's arguments, and reference() takes and returns one part's arrays. A program takes and returns all parts, laid end to end along the dimension named above; an argument that names none is the same for every part. Nothing has to cross between parts.
All inputs are finite; a program needn't handle non-finite values.
Results may differ from the reference program's by a relative error of at most 0.004.
Values may be sent and summed in bfloat16 or wider, within the bound.
No kernel may reach another device: no remote copies, remote signals or barrier semaphores. Data moves between devices by JAX's collectives and lax.ppermute only.
A program may use at most 64 MiB of HBM per device.

```python
import math
import jax
import jax.numpy as jnp
from jax import lax

D = 1152
HEADS = 20
HEAD_WIDTH = 32
FH = 8
FW = 32
HW = 640
NF = 64
TOKENS = 16384


def draw_tokens(key, part):
    key = jax.random.fold_in(key, 11)
    key_frame, key_noise, key_chan = jax.random.split(key, 3)
    frame_mean = jnp.clip(jax.random.normal(key_frame, (NF, 1, D), jnp.float32), -4.0, 4.0)
    ramp = (0.5 + jnp.arange(NF, dtype=jnp.float32) / max(NF - 1, 1)).reshape(NF, 1, 1)
    channel = jnp.exp(jax.random.uniform(key_chan, (1, 1, D), jnp.float32) * math.log(10.0))
    noise = jnp.clip(jax.random.normal(key_noise, (NF, FH * FW, D), jnp.float32), -4.0, 4.0)
    row_scale = jnp.ones((NF, FH * FW, 1), jnp.float32)
    inner = jnp.clip(ramp * frame_mean + noise, -10.0, 10.0)
    return (channel * row_scale * inner).reshape(TOKENS, D).astype(jnp.bfloat16)


def shard_levels(rng, shape, cuts, least, largest):
    def one(position, parts):
        steps = jax.random.uniform(jax.random.fold_in(jax.random.fold_in(rng, 6), position), (parts,), jnp.float32, least / len(cuts), largest / len(cuts))
        return jnp.repeat(jnp.exp(steps), shape[position] // parts).reshape((-1,) + (1,) * (len(shape) - position - 1))

    level = one(*cuts[0])
    for cut in cuts[1:]:
        level = level * one(*cut)
    return level


def scatter_about(key, shape, spread, reach, cuts=(), kind=jnp.bfloat16):
    loudness = shard_levels(key, shape, cuts, -0.22, 0.18) if cuts else 1.0
    values = jax.random.normal(key, shape, jnp.float32) * spread * loudness
    return jnp.minimum(jnp.maximum(values, -reach), reach).astype(kind)


def setup_inputs(seed: int = 0, part: int = 0) -> dict:
    streams_of = jax.random.split(jax.random.key(seed), 7)
    part_splits = jax.random.split(jax.random.fold_in(streams_of[6], part), 7)
    return {
        "tokens": draw_tokens(jax.random.fold_in(jax.random.fold_in(streams_of[6], part), 71), part),
        "gain": jnp.clip(1.0 + 0.18 * jax.random.normal(streams_of[1], (D,), jnp.float32), 0.099609375, 1.8984375).astype(jnp.bfloat16),
        "w_query": scatter_about(streams_of[2], (D, HW), (D // 9) ** -0.5, 0.5, ((0, 64),)),
        "w_key": scatter_about(streams_of[3], (D, HW), (D // 9) ** -0.5, 0.5, ((0, 64),)),
        "w_value": scatter_about(streams_of[4], (D, HW), D ** -0.5, 0.1875, ((0, 64),)),
        "conv_weight": scatter_about(streams_of[5], (27, HW), 27 ** -0.5, 1.25),
    }


def reference(tokens, gain, w_query, w_key, w_value, conv_weight):
    xfloat = tokens.astype(jnp.float32)
    scale = lax.rsqrt(lax.optimization_barrier(jnp.mean(xfloat * xfloat, axis=1, keepdims=True)) + 1e-06)
    normed = (xfloat * scale * gain.astype(jnp.float32)).astype(jnp.bfloat16)
    query = jnp.dot(normed, w_query, preferred_element_type=jnp.float32)
    keys = jnp.dot(normed, w_key, preferred_element_type=jnp.float32)
    values = jnp.dot(normed, w_value, preferred_element_type=jnp.float32).astype(jnp.bfloat16)
    qfeat = (jax.nn.elu(query) + 1.0).astype(jnp.bfloat16)
    kfeat = (jax.nn.elu(keys) + 1.0).astype(jnp.bfloat16)
    key_heads = kfeat.astype(jnp.float32).reshape(TOKENS, HEADS, HEAD_WIDTH)
    value_heads = values.astype(jnp.float32).reshape(TOKENS, HEADS, HEAD_WIDTH)
    key_value_state = jnp.einsum('gin,gil->inl', key_heads, value_heads, precision=lax.Precision.HIGHEST)
    ksum = lax.optimization_barrier(jnp.sum(key_heads, axis=0))
    query_heads = qfeat.astype(jnp.float32).reshape(TOKENS, HEADS, HEAD_WIDTH)
    numerator = jnp.einsum('dnb,nbt->dnt', query_heads, key_value_state, precision=lax.Precision.HIGHEST)
    denom = jnp.einsum('rhk,hk->rh', query_heads, ksum, precision=lax.Precision.HIGHEST)
    attended = (numerator / denom[:, :, None]).reshape(TOKENS, HW)
    volume = values.reshape(NF, FH, FW, HW)
    padded = jnp.pad(volume, ((1, 1), (1, 1), (1, 1), (0, 0)))
    kernel = conv_weight.astype(jnp.float32)
    local = jnp.zeros((NF, FH, FW, HW), jnp.float32)
    for shift_t in range(3):
        for shift_y in range(3):
            for shift_x in range(3):
                window = padded[shift_t:shift_t + NF, shift_y:shift_y + FH, shift_x:shift_x + FW, :]
                local = local + window.astype(jnp.float32) * kernel[9 * shift_t + 3 * shift_y + shift_x]
    return attended + local.reshape(TOKENS, HW)
```

```python
import jax
import jax.numpy as jnp
from jax import lax
from jax.sharding import Mesh
from jax.sharding import PartitionSpec as P

HEAD_WIDTH = 32
FH = 8
FW = 32
LANES = 128

AXES = ("y", "core", "x", "zh", "zl")
ZAX = ("zh", "zl")
TM = ("x", "zh", "zl")
NEAR = ("x", "zl")


def exchange(blocks, axes):
    return lax.all_to_all(blocks, axes, 0, 0, tiled=True)


def spread(block, axes):
    count = lax.axis_size(axes)
    return exchange(jnp.broadcast_to(block[None], (count,) + block.shape), axes)


def swap(block):
    return lax.ppermute(block, "core", [(0, 1), (1, 0)])


def gather_weights(w_query, w_key, w_value):
    rows = w_query.shape[0]
    pad = jnp.zeros((rows, LANES), w_query.dtype)
    first = jnp.concatenate([w_value, w_query[:, : 3 * LANES]], axis=1)
    second = jnp.concatenate([w_key, w_query[:, 3 * LANES :], pad], axis=1)
    core = lax.axis_index("core")
    mine = jnp.where(core == 0, first, second)
    mine = lax.dynamic_slice_in_dim(mine, lax.axis_index("y") * 2 * LANES, 2 * LANES, axis=1)
    column = spread(mine, ZAX)
    column = column.reshape(column.shape[0] * rows, 2 * LANES)
    full = spread(column, ("y", "x"))
    return full.reshape(lax.axis_size("y"), -1, 2 * LANES)


def body(tokens, gain, w_query, w_key, w_value, conv_weight):
    rows = tokens.shape[0]
    width = w_query.shape[1]
    heads = width // HEAD_WIDTH
    groups = width // LANES
    core = lax.axis_index("core")
    xfloat = tokens.astype(jnp.float32)
    scale = lax.rsqrt(jnp.mean(xfloat * xfloat, axis=1, keepdims=True) + 1e-06)
    normed = (xfloat * scale * gain.astype(jnp.float32)).astype(jnp.bfloat16)
    other = swap(normed)
    weights = gather_weights(w_query, w_key, w_value)
    both = jnp.concatenate([normed, other], axis=0)
    proj = jnp.concatenate(
        [jnp.dot(both, weights[i], preferred_element_type=jnp.float32) for i in range(weights.shape[0])],
        axis=1,
    )
    feat = jax.nn.elu(proj) + 1.0
    plain = jnp.logical_and(core == 0, lax.broadcasted_iota(jnp.int32, proj.shape, 1) < width)
    proj = jnp.where(plain, proj, feat).astype(jnp.bfloat16)
    mine, theirs = proj[:rows], swap(proj[rows:])
    first = jnp.where(core == 0, mine, theirs)
    second = jnp.where(core == 0, theirs, mine)
    values = first[:, :width]
    kfeat = second[:, :width]
    qfeat = jnp.concatenate([first[:, width:], second[:, width : 2 * width - 3 * LANES]], axis=1)

    count = lax.axis_size(TM)
    before = lax.ppermute(values, TM, [(i, i + 1) for i in range(count - 1)])
    after = lax.ppermute(values, TM, [(i + 1, i) for i in range(count - 1)])

    state = jnp.einsum(
        "gni,gnl->inl",
        kfeat.reshape(rows, heads, HEAD_WIDTH),
        values.reshape(rows, heads, HEAD_WIDTH),
        preferred_element_type=jnp.float32,
    ).reshape(HEAD_WIDTH, width)
    ksum = jnp.sum(kfeat, axis=0, dtype=jnp.float32)
    near = lax.axis_size(NEAR)
    chunks = jnp.concatenate([state.reshape(near, -1), ksum.reshape(near, -1)], axis=1)
    part = jnp.sum(exchange(chunks, NEAR), axis=0)
    part = jnp.sum(spread(part, "zh"), axis=0)
    chunks = spread(part, NEAR)
    state = chunks[:, : HEAD_WIDTH * width // near].reshape(HEAD_WIDTH, heads, HEAD_WIDTH)
    ksum = chunks[:, HEAD_WIDTH * width // near :].reshape(heads, HEAD_WIDTH)

    framed = jnp.stack([before, values, after]).reshape(3, FH, FW, width)
    padded = jnp.pad(framed, ((0, 0), (1, 1), (1, 1), (0, 0)))
    kernel = conv_weight.astype(jnp.float32)
    local = jnp.zeros((FH, FW, width), jnp.float32)
    for shift_t in range(3):
        for shift_y in range(3):
            for shift_x in range(3):
                window = padded[shift_t, shift_y : shift_y + FH, shift_x : shift_x + FW, :]
                local = (
                    local + window.astype(jnp.float32) * kernel[9 * shift_t + 3 * shift_y + shift_x]
                )
    query_heads = qfeat.astype(jnp.float32).reshape(rows, heads, HEAD_WIDTH)
    numerator = jnp.einsum("dnb,bnt->dnt", query_heads, state, precision=lax.Precision.HIGHEST)
    denom = jnp.einsum("rhk,hk->rh", query_heads, ksum, precision=lax.Precision.HIGHEST)
    attended = (numerator / denom[:, :, None]).reshape(rows, width)
    return attended + local.reshape(rows, width)


def solution(mesh):
    fine = Mesh(mesh.devices.reshape(4, 2, 4, 4, 4), AXES)
    rows = P(AXES, None)
    split = P(TM, None)
    return jax.shard_map(
        body, mesh=fine, in_specs=(rows, P(), split, split, split, P()), out_specs=rows, check_vma=False
    )
```

```python
import jax
import jax.numpy as jnp
from jax import lax
from jax.experimental import pallas as pl
from jax.experimental.pallas import tpu as pltpu
from jax.sharding import Mesh
from jax.sharding import PartitionSpec as P

HEAD_WIDTH = 32
FH = 8
FW = 32
LANES = 128
BLOCK = 2 * LANES
GROUPS = 5
TILES = 32

AXES = ("y", "core", "x", "zh", "zl")
ZAX = ("zh", "zl")
TM = ("x", "zh", "zl")
NEAR = ("x", "zl")
PARAMS = pltpu.CompilerParams(vmem_limit_bytes=40 * 1024 * 1024)


def cost(flops, nbytes):
    return pl.CostEstimate(flops=flops, bytes_accessed=nbytes, transcendentals=0)


def exchange(blocks, axes):
    return lax.all_to_all(blocks, axes, 0, 0, tiled=True)


def spread(block, axes):
    count = lax.axis_size(axes)
    return exchange(jnp.broadcast_to(block[None], (count,) + block.shape), axes)


def norm_kernel(tokens_ref, gain_ref, out_ref):
    x = tokens_ref[...].astype(jnp.float32)
    scale = lax.rsqrt(jnp.mean(x * x, axis=1, keepdims=True) + 1e-06)
    normed = (x * scale * gain_ref[...].astype(jnp.float32)).astype(jnp.bfloat16)
    for i in range(out_ref.shape[0]):
        out_ref[i] = normed


def norm(tokens, gain, copies):
    return pl.pallas_call(
        norm_kernel,
        out_shape=jax.ShapeDtypeStruct((copies,) + tokens.shape, jnp.bfloat16),
        compiler_params=PARAMS,
        cost_estimate=cost(10 * tokens.size, 10 * tokens.size),
        name="norm",
    )(tokens, gain.reshape(1, -1))


def project_kernel(tokens_ref, mine_ref, theirs_ref, out_ref):
    core = lax.axis_index("core")
    first = lax.axis_index("y") * 4
    tokens = tokens_ref[0]
    for half, ref in enumerate((mine_ref, theirs_ref)):
        place = core if half == 0 else 1 - core
        proj = jnp.dot(tokens, ref[...], preferred_element_type=jnp.float32)
        feat = jnp.where(proj > 0, proj, jnp.exp(jnp.minimum(proj, 0.0)) - 1.0) + 1.0
        lane = lax.broadcasted_iota(jnp.int32, proj.shape, 1)
        unit = first + 2 * place + lane // LANES
        proj = jnp.where(unit < GROUPS, proj, feat).astype(jnp.bfloat16)
        out_ref[0, :, pl.ds(pl.multiple_of(place * BLOCK, BLOCK), BLOCK)] = proj


def project(tokens, mine, theirs):
    videos, rows, depth = tokens.shape
    whole = pl.BlockSpec((depth, BLOCK), lambda i: (0, 0))
    return pl.pallas_call(
        project_kernel,
        grid=(videos,),
        in_specs=[pl.BlockSpec((1, rows, depth), lambda i: (i, 0, 0)), whole, whole],
        out_specs=pl.BlockSpec((1, rows, 2 * BLOCK), lambda i: (i, 0, 0)),
        out_shape=jax.ShapeDtypeStruct((videos, rows, 2 * BLOCK), jnp.bfloat16),
        compiler_params=PARAMS,
        cost_estimate=cost(2 * videos * rows * depth * 2 * BLOCK, 4 * 1024 * 1024),
        name="project",
    )(tokens, mine, theirs)


def unit_of(ref, unit):
    at = unit % 4
    return ref[unit // 4, :, at * LANES : (at + 1) * LANES]


def state_kernel(proj_ref, values_ref, tiles_ref):
    lane = lax.broadcasted_iota(jnp.int32, (HEAD_WIDTH, LANES), 1) // HEAD_WIDTH
    tiles_ref[...] = jnp.zeros_like(tiles_ref)
    for g in range(GROUPS):
        values = unit_of(proj_ref, g)
        kfeat = unit_of(proj_ref, GROUPS + g)
        values_ref[:, g * LANES : (g + 1) * LANES] = values
        square = lax.dot_general(
            kfeat, values, (((0,), (0,)), ((), ())), preferred_element_type=jnp.float32
        )
        packed = jnp.zeros((HEAD_WIDTH, LANES), jnp.float32)
        for h in range(LANES // HEAD_WIDTH):
            packed = jnp.where(lane == h, square[h * HEAD_WIDTH : (h + 1) * HEAD_WIDTH], packed)
        for t in range(4):
            tiles_ref[4 * g + t] = packed[8 * t : 8 * t + 8]
        tiles_ref[4 * GROUPS, g : g + 1, :] = jnp.sum(
            kfeat.astype(jnp.float32), axis=0, keepdims=True
        )


def states(proj):
    rows = proj.shape[1]
    return pl.pallas_call(
        state_kernel,
        out_shape=(
            jax.ShapeDtypeStruct((rows, GROUPS * LANES), jnp.bfloat16),
            jax.ShapeDtypeStruct((TILES, 8, LANES), jnp.float32),
        ),
        compiler_params=PARAMS,
        cost_estimate=cost(2 * rows * GROUPS * LANES * LANES, 2 * 1024 * 1024),
        name="states",
    )(proj)


def conv_kernel(before_ref, values_ref, after_ref, weight_ref, out_ref):
    zeros = jnp.zeros((FW, LANES), jnp.float32)
    rows = FH * FW
    x = lax.broadcasted_iota(jnp.int32, (rows, LANES), 0) % FW
    weight = weight_ref[...].astype(jnp.float32)
    frames = [
        jnp.concatenate([zeros, ref[...].astype(jnp.float32), zeros], axis=0)
        for ref in (before_ref, values_ref, after_ref)
    ]
    sums = []
    for c in range(3):
        total = None
        for a in range(3):
            for b in range(3):
                tap = 9 * a + 3 * b + c
                term = frames[a][b * FW : b * FW + rows] * weight[tap : tap + 1]
                total = term if total is None else total + term
        sums.append(total)
    left = jnp.where(x == 0, 0.0, pltpu.roll(sums[0], 1, 0))
    right = jnp.where(x == FW - 1, 0.0, pltpu.roll(sums[2], rows - 1, 0))
    out_ref[...] = left + sums[1] + right


def convolve(before, values, after, weight):
    rows, width = values.shape
    block = pl.BlockSpec((rows, LANES), lambda i: (0, i))
    return pl.pallas_call(
        conv_kernel,
        grid=(width // LANES,),
        in_specs=[block, block, block, pl.BlockSpec((27, LANES), lambda i: (0, i))],
        out_specs=block,
        out_shape=jax.ShapeDtypeStruct((rows, width), jnp.float32),
        compiler_params=PARAMS,
        cost_estimate=cost(54 * rows * width, 2 * 1024 * 1024),
        name="convolve",
    )(before, values, after, weight)


def split_dot(a, b):
    high = b.astype(jnp.bfloat16)
    low = (b - high.astype(jnp.float32)).astype(jnp.bfloat16)
    return jnp.dot(a, high, preferred_element_type=jnp.float32) + jnp.dot(
        a, low, preferred_element_type=jnp.float32
    )


def attend_kernel(proj_ref, tiles_ref, local_ref, out_ref):
    row = lax.broadcasted_iota(jnp.int32, (LANES, LANES), 0) // HEAD_WIDTH
    lane = lax.broadcasted_iota(jnp.int32, (LANES, LANES), 1) // HEAD_WIDTH
    same = row == lane
    for g in range(GROUPS):
        qfeat = unit_of(proj_ref, 2 * GROUPS + g)
        packed = tiles_ref[4 * g : 4 * g + 4].reshape(HEAD_WIDTH, LANES)
        state = jnp.where(same, jnp.concatenate([packed] * 4, axis=0), 0.0)
        ksum = jnp.broadcast_to(tiles_ref[4 * GROUPS, g : g + 1, :], (LANES, LANES)).T
        ksum = jnp.where(same, ksum, 0.0)
        both = split_dot(qfeat, jnp.concatenate([state, ksum], axis=1))
        cols = slice(g * LANES, (g + 1) * LANES)
        out_ref[:, cols] = both[:, :LANES] / both[:, LANES:] + local_ref[:, cols]


def attend(proj, tiles, local):
    rows, width = local.shape
    return pl.pallas_call(
        attend_kernel,
        out_shape=jax.ShapeDtypeStruct((rows, width), jnp.float32),
        compiler_params=PARAMS,
        cost_estimate=cost(8 * rows * width * LANES, 3 * 1024 * 1024),
        name="attend",
    )(proj, tiles, local)


def gather_weights(w_query, w_key, w_value):
    rows = w_query.shape[0]
    pad = jnp.zeros((rows, LANES), w_query.dtype)
    cat = jnp.concatenate([w_value, w_key, w_query, pad], axis=1)
    place = 2 * lax.axis_index("y") + lax.axis_index("core")
    mine = lax.dynamic_slice_in_dim(cat, place * BLOCK, BLOCK, axis=1)
    column = spread(mine, ZAX)
    column = column.reshape(column.shape[0] * rows, BLOCK)
    return spread(column, "x").reshape(-1, BLOCK)


def total_state(tiles):
    near = lax.axis_size(NEAR)
    shape = (near, TILES // near) + tiles.shape[1:]
    part = jnp.sum(exchange(tiles, NEAR).reshape(shape), axis=0)
    part = jnp.sum(spread(part, "zh"), axis=0)
    return spread(part, NEAR).reshape(tiles.shape)


def body(tokens, gain, w_query, w_key, w_value, conv_weight):
    mine = gather_weights(w_query, w_key, w_value)
    theirs = lax.ppermute(mine, "core", [(0, 1), (1, 0)])
    normed = exchange(norm(tokens, gain, lax.axis_size("y")), "y")
    proj = exchange(project(normed, mine, theirs), "y")
    values, tiles = states(proj)
    count = lax.axis_size(TM)
    before = lax.ppermute(values, TM, [(i, i + 1) for i in range(count - 1)])
    after = lax.ppermute(values, TM, [(i + 1, i) for i in range(count - 1)])
    tiles = total_state(tiles)
    local = convolve(before, values, after, conv_weight)
    return attend(proj, tiles, local)


def solution(mesh):
    fine = Mesh(mesh.devices.reshape(4, 2, 4, 4, 4), AXES)
    rows = P(AXES, None)
    split = P(TM, None)
    return jax.shard_map(
        body, mesh=fine, in_specs=(rows, P(), split, split, split, P()), out_specs=rows, check_vma=False
    )
```

```python
import jax
import jax.numpy as jnp
from jax import lax
from jax.experimental import pallas as pl
from jax.experimental.pallas import tpu as pltpu
from jax.sharding import Mesh
from jax.sharding import PartitionSpec as P

HEAD_WIDTH = 32
FH = 8
FW = 32
LANES = 128
BLOCK = 2 * LANES
GROUPS = 5
TILES = 32

AXES = ("y", "core", "x", "zh", "zl")
ZAX = ("zh", "zl")
TM = ("x", "zh", "zl")
NEAR = ("x", "zl")
PARAMS = pltpu.CompilerParams(vmem_limit_bytes=40 * 1024 * 1024)


def cost(flops, nbytes):
    return pl.CostEstimate(flops=flops, bytes_accessed=nbytes, transcendentals=0)


def exchange(blocks, axes):
    return lax.all_to_all(blocks, axes, 0, 0, tiled=True)


def spread(block, axes):
    count = lax.axis_size(axes)
    return exchange(jnp.broadcast_to(block[None], (count,) + block.shape), axes)


def norm_kernel(tokens_ref, gain_ref, out_ref):
    x = tokens_ref[...].astype(jnp.float32)
    scale = lax.rsqrt(jnp.mean(x * x, axis=1, keepdims=True) + 1e-06)
    out_ref[...] = (x * scale * gain_ref[...].astype(jnp.float32)).astype(jnp.bfloat16)


def norm(tokens, gain):
    return pl.pallas_call(
        norm_kernel,
        out_shape=jax.ShapeDtypeStruct(tokens.shape, jnp.bfloat16),
        compiler_params=PARAMS,
        cost_estimate=cost(10 * tokens.size, 4 * tokens.size),
        name="norm",
    )(tokens, gain.reshape(1, -1))


def project_kernel(mine_ref, theirs_ref, weight_ref, *out_refs):
    core = lax.axis_index("core")
    weight = weight_ref[0]
    split = GROUPS * LANES
    for tokens_ref, main_ref, rest_ref in (
        (mine_ref, out_refs[0], out_refs[1]),
        (theirs_ref, out_refs[2], out_refs[3]),
    ):
        proj = jnp.dot(tokens_ref[...], weight, preferred_element_type=jnp.float32)
        feat = jnp.where(proj > 0, proj, jnp.exp(jnp.minimum(proj, 0.0)) - 1.0) + 1.0
        unit = 2 * pl.program_id(0) + lax.broadcasted_iota(jnp.int32, proj.shape, 1) // LANES
        plain = jnp.logical_and(unit < GROUPS, core == 0)
        proj = jnp.where(plain, proj, feat).astype(jnp.bfloat16)
        for step in range(4):

            @pl.when(pl.program_id(0) == step)
            def _():
                for half in range(2):
                    at = step * BLOCK + half * LANES
                    ref = main_ref if at < split else rest_ref
                    at = at if at < split else at - split
                    ref[:, at : at + LANES] = proj[:, half * LANES : (half + 1) * LANES]


def project(mine, theirs, weights):
    steps, depth, _ = weights.shape
    rows = mine.shape[0]
    widths = (GROUPS * LANES, steps * BLOCK - GROUPS * LANES) * 2
    tokens = pl.BlockSpec((rows, depth), lambda i: (0, 0))
    return pl.pallas_call(
        project_kernel,
        grid=(steps,),
        in_specs=[tokens, tokens, pl.BlockSpec((1, depth, BLOCK), lambda i: (i, 0, 0))],
        out_specs=[pl.BlockSpec((rows, width), lambda i: (0, 0)) for width in widths],
        out_shape=[jax.ShapeDtypeStruct((rows, width), jnp.bfloat16) for width in widths],
        compiler_params=PARAMS,
        cost_estimate=cost(4 * rows * depth * steps * BLOCK, 5 * 1024 * 1024),
        name="project",
    )(mine, theirs, weights)


def state_kernel(mine_ref, theirs_ref, values_ref, tiles_ref):
    first = lax.axis_index("core") == 0
    lane = lax.broadcasted_iota(jnp.int32, (HEAD_WIDTH, LANES), 1) // HEAD_WIDTH
    tiles_ref[...] = jnp.zeros_like(tiles_ref)
    for g in range(GROUPS):
        cols = slice(g * LANES, (g + 1) * LANES)
        values = jnp.where(first, mine_ref[:, cols], theirs_ref[:, cols])
        kfeat = jnp.where(first, theirs_ref[:, cols], mine_ref[:, cols])
        values_ref[:, cols] = values
        square = lax.dot_general(
            kfeat, values, (((0,), (0,)), ((), ())), preferred_element_type=jnp.float32
        )
        packed = jnp.zeros((HEAD_WIDTH, LANES), jnp.float32)
        for h in range(LANES // HEAD_WIDTH):
            packed = jnp.where(lane == h, square[h * HEAD_WIDTH : (h + 1) * HEAD_WIDTH], packed)
        for t in range(4):
            tiles_ref[4 * g + t] = packed[8 * t : 8 * t + 8]
        tiles_ref[4 * GROUPS, g : g + 1, :] = jnp.sum(
            kfeat.astype(jnp.float32), axis=0, keepdims=True
        )


def states(mine, theirs):
    rows = mine.shape[0]
    return pl.pallas_call(
        state_kernel,
        out_shape=(
            jax.ShapeDtypeStruct((rows, GROUPS * LANES), jnp.bfloat16),
            jax.ShapeDtypeStruct((TILES, 8, LANES), jnp.float32),
        ),
        compiler_params=PARAMS,
        cost_estimate=cost(2 * rows * GROUPS * LANES * LANES, 2 * 1024 * 1024),
        name="states",
    )(mine, theirs)


def conv_kernel(before_ref, values_ref, after_ref, weight_ref, out_ref):
    zeros = jnp.zeros((FW, LANES), jnp.float32)
    rows = FH * FW
    x = lax.broadcasted_iota(jnp.int32, (rows, LANES), 0) % FW
    weight = weight_ref[...].astype(jnp.float32)
    frames = [
        jnp.concatenate([zeros, ref[...].astype(jnp.float32), zeros], axis=0)
        for ref in (before_ref, values_ref, after_ref)
    ]
    sums = []
    for c in range(3):
        total = None
        for a in range(3):
            for b in range(3):
                tap = 9 * a + 3 * b + c
                term = frames[a][b * FW : b * FW + rows] * weight[tap : tap + 1]
                total = term if total is None else total + term
        sums.append(total)
    left = jnp.where(x == 0, 0.0, pltpu.roll(sums[0], 1, 0))
    right = jnp.where(x == FW - 1, 0.0, pltpu.roll(sums[2], rows - 1, 0))
    out_ref[...] = left + sums[1] + right


def convolve(before, values, after, weight):
    rows, width = values.shape
    block = pl.BlockSpec((rows, LANES), lambda i: (0, i))
    return pl.pallas_call(
        conv_kernel,
        grid=(width // LANES,),
        in_specs=[block, block, block, pl.BlockSpec((27, LANES), lambda i: (0, i))],
        out_specs=block,
        out_shape=jax.ShapeDtypeStruct((rows, width), jnp.float32),
        compiler_params=PARAMS,
        cost_estimate=cost(54 * rows * width, 2 * 1024 * 1024),
        name="convolve",
    )(before, values, after, weight)


def split_dot(a, b):
    high = b.astype(jnp.bfloat16)
    low = (b - high.astype(jnp.float32)).astype(jnp.bfloat16)
    return jnp.dot(a, high, preferred_element_type=jnp.float32) + jnp.dot(
        a, low, preferred_element_type=jnp.float32
    )


def attend_kernel(mine_ref, theirs_ref, tiles_ref, local_ref, out_ref):
    first = lax.axis_index("core") == 0
    row = lax.broadcasted_iota(jnp.int32, (LANES, LANES), 0) // HEAD_WIDTH
    lane = lax.broadcasted_iota(jnp.int32, (LANES, LANES), 1) // HEAD_WIDTH
    same = row == lane
    for g in range(GROUPS):
        early, late = (mine_ref, theirs_ref) if g < 3 else (theirs_ref, mine_ref)
        at = slice(g % 3 * LANES, (g % 3 + 1) * LANES)
        qfeat = jnp.where(first, early[:, at], late[:, at])
        packed = tiles_ref[4 * g : 4 * g + 4].reshape(HEAD_WIDTH, LANES)
        state = jnp.where(same, jnp.concatenate([packed] * 4, axis=0), 0.0)
        ksum = jnp.broadcast_to(tiles_ref[4 * GROUPS, g : g + 1, :], (LANES, LANES)).T
        ksum = jnp.where(same, ksum, 0.0)
        both = split_dot(qfeat, jnp.concatenate([state, ksum], axis=1))
        cols = slice(g * LANES, (g + 1) * LANES)
        out_ref[:, cols] = both[:, :LANES] / both[:, LANES:] + local_ref[:, cols]


def attend(mine, theirs, tiles, local):
    rows, width = local.shape
    return pl.pallas_call(
        attend_kernel,
        out_shape=jax.ShapeDtypeStruct((rows, width), jnp.float32),
        compiler_params=PARAMS,
        cost_estimate=cost(8 * rows * width * LANES, 3 * 1024 * 1024),
        name="attend",
    )(mine, theirs, tiles, local)


def swap(block):
    return lax.ppermute(block, "core", [(0, 1), (1, 0)])


def gather_weights(w_query, w_key, w_value):
    rows = w_query.shape[0]
    pad = jnp.zeros((rows, LANES), w_query.dtype)
    cut = 3 * LANES
    cat = jnp.concatenate([w_value, w_query[:, :cut], w_key, w_query[:, cut:], pad], axis=1)
    place = 4 * lax.axis_index("core") + lax.axis_index("y")
    mine = lax.dynamic_slice_in_dim(cat, place * BLOCK, BLOCK, axis=1)
    mine = jnp.concatenate([mine[:, :LANES], mine[:, LANES:]], axis=0)
    column = spread(mine, ZAX)
    column = jnp.concatenate([column[:, :rows], column[:, rows:]], axis=2)
    column = column.reshape(column.shape[0] * rows, BLOCK)
    return spread(column, ("y", "x")).reshape(lax.axis_size("y"), -1, BLOCK)


def body(tokens, gain, w_query, w_key, w_value, conv_weight):
    normed = norm(tokens, gain)
    weights = gather_weights(w_query, w_key, w_value)
    main, rest, their_main, their_rest = project(normed, swap(normed), weights)
    values, tiles = states(main, swap(their_main))
    their_rest = swap(their_rest)
    count = lax.axis_size(TM)
    before = lax.ppermute(values, TM, [(i, i + 1) for i in range(count - 1)])
    after = lax.ppermute(values, TM, [(i + 1, i) for i in range(count - 1)])
    local = convolve(before, values, after, conv_weight)

    near = lax.axis_size(NEAR)
    shape = (near, TILES // near) + tiles.shape[1:]
    part = jnp.sum(exchange(tiles, NEAR).reshape(shape), axis=0)
    part = jnp.sum(spread(part, "zh"), axis=0)
    part, local = lax.optimization_barrier((part, local))
    tiles = spread(part, NEAR).reshape(tiles.shape)
    return attend(rest, their_rest, tiles, local)


def solution(mesh):
    fine = Mesh(mesh.devices.reshape(4, 2, 4, 4, 4), AXES)
    rows = P(AXES, None)
    split = P(TM, None)
    return jax.shard_map(
        body, mesh=fine, in_specs=(rows, P(), split, split, split, P()), out_specs=rows, check_vma=False
    )
```

```python
import jax
import jax.numpy as jnp
from jax import lax
from jax.experimental import pallas as pl
from jax.experimental.pallas import tpu as pltpu
from jax.sharding import Mesh
from jax.sharding import PartitionSpec as P

HEAD_WIDTH = 32
FH = 8
FW = 32
LANES = 128
BLOCK = 2 * LANES
GROUPS = 5
TILES = 24

AXES = ("y", "core", "x", "zh", "zl")
ZAX = ("zh", "zl")
TM = ("x", "zh", "zl")
PARAMS = pltpu.CompilerParams(vmem_limit_bytes=16 * 1024 * 1024)


def cost(flops, nbytes):
    return pl.CostEstimate(flops=flops, bytes_accessed=nbytes, transcendentals=0)


def exchange(blocks, axes):
    return lax.all_to_all(blocks, axes, 0, 0, tiled=True)


def spread(block, axes):
    count = lax.axis_size(axes)
    return exchange(jnp.broadcast_to(block[None], (count,) + block.shape), axes)


def norm_kernel(tokens_ref, gain_ref, out_ref):
    x = tokens_ref[...].astype(jnp.float32)
    scale = lax.rsqrt(jnp.mean(x * x, axis=1, keepdims=True) + 1e-06)
    out_ref[...] = (x * scale * gain_ref[...].astype(jnp.float32)).astype(jnp.bfloat16)


def norm(tokens, gain):
    return pl.pallas_call(
        norm_kernel,
        out_shape=jax.ShapeDtypeStruct(tokens.shape, jnp.bfloat16),
        compiler_params=PARAMS,
        cost_estimate=cost(10 * tokens.size, 4 * tokens.size),
        name="norm",
    )(tokens, gain.reshape(1, -1))


def project_kernel(mine_ref, theirs_ref, weight_ref, *out_refs):
    first = lax.axis_index("core") == 0
    split = GROUPS * LANES
    for step in range(weight_ref.shape[0]):
        weight = weight_ref[step]
        for tokens_ref, main_ref, rest_ref in (
            (mine_ref, out_refs[0], out_refs[1]),
            (theirs_ref, out_refs[2], out_refs[3]),
        ):
            both = jnp.dot(tokens_ref[...], weight, preferred_element_type=jnp.float32)
            for half in range(2):
                at = step * BLOCK + half * LANES
                proj = both[:, half * LANES : (half + 1) * LANES]
                feat = jnp.where(proj > 0, proj, jnp.exp(jnp.minimum(proj, 0.0)) - 1.0) + 1.0
                if at < split:
                    feat = jnp.where(first, proj, feat).astype(jnp.bfloat16)
                    main_ref[:, at : at + LANES] = feat
                else:
                    rest_ref[:, at - split : at - split + LANES] = feat.astype(jnp.bfloat16)


def project(mine, theirs, weights):
    steps, depth, _ = weights.shape
    rows = mine.shape[0]
    widths = (GROUPS * LANES, steps * BLOCK - GROUPS * LANES) * 2
    return pl.pallas_call(
        project_kernel,
        out_shape=[jax.ShapeDtypeStruct((rows, width), jnp.bfloat16) for width in widths],
        compiler_params=PARAMS,
        cost_estimate=cost(4 * rows * depth * steps * BLOCK, 5 * 1024 * 1024),
        name="project",
    )(mine, theirs, weights)


def state_kernel(mine_ref, theirs_ref, values_ref, tiles_ref):
    first = lax.axis_index("core") == 0
    lane = lax.broadcasted_iota(jnp.int32, (HEAD_WIDTH, LANES), 1) // HEAD_WIDTH
    tiles_ref[...] = jnp.zeros_like(tiles_ref)
    for g in range(GROUPS):
        cols = slice(g * LANES, (g + 1) * LANES)
        values = jnp.where(first, mine_ref[:, cols], theirs_ref[:, cols])
        kfeat = jnp.where(first, theirs_ref[:, cols], mine_ref[:, cols])
        values_ref[:, cols] = values
        square = lax.dot_general(
            kfeat, values, (((0,), (0,)), ((), ())), preferred_element_type=jnp.float32
        )
        packed = jnp.zeros((HEAD_WIDTH, LANES), jnp.float32)
        for h in range(LANES // HEAD_WIDTH):
            packed = jnp.where(lane == h, square[h * HEAD_WIDTH : (h + 1) * HEAD_WIDTH], packed)
        for t in range(4):
            tiles_ref[4 * g + t] = packed[8 * t : 8 * t + 8]
        tiles_ref[4 * GROUPS, g : g + 1, :] = jnp.sum(
            kfeat.astype(jnp.float32), axis=0, keepdims=True
        )


def states(mine, theirs):
    rows = mine.shape[0]
    return pl.pallas_call(
        state_kernel,
        out_shape=(
            jax.ShapeDtypeStruct((rows, GROUPS * LANES), jnp.bfloat16),
            jax.ShapeDtypeStruct((TILES, 8, LANES), jnp.float32),
        ),
        compiler_params=PARAMS,
        cost_estimate=cost(2 * rows * GROUPS * LANES * LANES, 2 * 1024 * 1024),
        name="states",
    )(mine, theirs)


def conv_kernel(before_ref, values_ref, after_ref, weight_ref, out_ref):
    zeros = jnp.zeros((FW, LANES), jnp.float32)
    rows = FH * FW
    x = lax.broadcasted_iota(jnp.int32, (rows, LANES), 0) % FW
    weight = weight_ref[...].astype(jnp.float32)
    frames = [
        jnp.concatenate([zeros, ref[...].astype(jnp.float32), zeros], axis=0)
        for ref in (before_ref, values_ref, after_ref)
    ]
    sums = []
    for c in range(3):
        total = None
        for a in range(3):
            for b in range(3):
                tap = 9 * a + 3 * b + c
                term = frames[a][b * FW : b * FW + rows] * weight[tap : tap + 1]
                total = term if total is None else total + term
        sums.append(total)
    left = jnp.where(x == 0, 0.0, pltpu.roll(sums[0], 1, 0))
    right = jnp.where(x == FW - 1, 0.0, pltpu.roll(sums[2], rows - 1, 0))
    out_ref[...] = left + sums[1] + right


def convolve(before, values, after, weight):
    rows, width = values.shape
    block = pl.BlockSpec((rows, LANES), lambda i: (0, i))
    return pl.pallas_call(
        conv_kernel,
        grid=(width // LANES,),
        in_specs=[block, block, block, pl.BlockSpec((27, LANES), lambda i: (0, i))],
        out_specs=block,
        out_shape=jax.ShapeDtypeStruct((rows, width), jnp.float32),
        compiler_params=PARAMS,
        cost_estimate=cost(54 * rows * width, 2 * 1024 * 1024),
        name="convolve",
    )(before, values, after, weight)


def split_dot(a, b):
    high = b.astype(jnp.bfloat16)
    low = (b - high.astype(jnp.float32)).astype(jnp.bfloat16)
    return jnp.dot(a, high, preferred_element_type=jnp.float32) + jnp.dot(
        a, low, preferred_element_type=jnp.float32
    )


def attend_kernel(mine_ref, theirs_ref, tiles_ref, local_ref, out_ref):
    first = lax.axis_index("core") == 0
    row = lax.broadcasted_iota(jnp.int32, (LANES, LANES), 0) // HEAD_WIDTH
    lane = lax.broadcasted_iota(jnp.int32, (LANES, LANES), 1) // HEAD_WIDTH
    same = row == lane
    for g in range(GROUPS):
        early, late = (mine_ref, theirs_ref) if g < 3 else (theirs_ref, mine_ref)
        at = slice(g % 3 * LANES, (g % 3 + 1) * LANES)
        qfeat = jnp.where(first, early[:, at], late[:, at])
        packed = tiles_ref[4 * g : 4 * g + 4].reshape(HEAD_WIDTH, LANES)
        state = jnp.where(same, jnp.concatenate([packed] * 4, axis=0), 0.0)
        ksum = jnp.broadcast_to(tiles_ref[4 * GROUPS, g : g + 1, :], (LANES, LANES)).T
        ksum = jnp.where(same, ksum, 0.0)
        both = split_dot(qfeat, jnp.concatenate([state, ksum], axis=1))
        cols = slice(g * LANES, (g + 1) * LANES)
        out_ref[:, cols] = both[:, :LANES] / both[:, LANES:] + local_ref[:, cols]


def attend(mine, theirs, tiles, local):
    rows, width = local.shape
    return pl.pallas_call(
        attend_kernel,
        out_shape=jax.ShapeDtypeStruct((rows, width), jnp.float32),
        compiler_params=PARAMS,
        cost_estimate=cost(8 * rows * width * LANES, 3 * 1024 * 1024),
        name="attend",
    )(mine, theirs, tiles, local)


def swap(block):
    return lax.ppermute(block, "core", [(0, 1), (1, 0)])


def pick_kernel(value_ref, key_ref, query_ref, out_ref, held):
    width = GROUPS * LANES
    cut = 3 * LANES
    query = query_ref[...].astype(jnp.float32)
    held[:, :width] = value_ref[...].astype(jnp.float32)
    held[:, width : width + cut] = query[:, :cut]
    held[:, width + cut : 2 * width + cut] = key_ref[...].astype(jnp.float32)
    held[:, 2 * width + cut : 3 * width] = query[:, cut:]
    held[:, 3 * width :] = jnp.zeros((held.shape[0], LANES), jnp.float32)
    place = 4 * lax.axis_index("core") + lax.axis_index("y")
    mine = held[:, pl.ds(pl.multiple_of(place * BLOCK, BLOCK), BLOCK)]
    mine = jnp.concatenate([mine[:, :LANES], mine[:, LANES:]], axis=0).astype(jnp.bfloat16)
    for i in range(out_ref.shape[0]):
        out_ref[i] = mine


def pick(w_value, w_key, w_query, copies):
    rows, width = w_query.shape
    return pl.pallas_call(
        pick_kernel,
        out_shape=jax.ShapeDtypeStruct((copies, 2 * rows, LANES), jnp.bfloat16),
        scratch_shapes=[pltpu.VMEM((rows, 3 * width + LANES), jnp.float32)],
        compiler_params=PARAMS,
        cost_estimate=cost(0, 4 * 1024 * rows),
        name="pick",
    )(w_value, w_key, w_query)


def body(tokens, gain, w_query, w_key, w_value, conv_weight):
    rows = w_query.shape[0]
    normed = norm(tokens, gain)
    other = swap(normed)
    column = exchange(pick(w_value, w_key, w_query, lax.axis_size(ZAX)), ZAX)
    column = jnp.concatenate([column[:, :rows], column[:, rows:]], axis=2).reshape(-1, BLOCK)
    column, other = lax.optimization_barrier((column, other))
    weights = spread(column, ("y", "x")).reshape(lax.axis_size("y"), -1, BLOCK)

    main, rest, their_main, their_rest = project(normed, other, weights)
    values, tiles = states(main, swap(their_main))
    their_rest = swap(their_rest)
    count = lax.axis_size(TM)
    before = lax.ppermute(values, TM, [(i, i + 1) for i in range(count - 1)])
    after = lax.ppermute(values, TM, [(i + 1, i) for i in range(count - 1)])
    local = convolve(before, values, after, conv_weight)

    share = TILES // lax.axis_size("x")
    part = jnp.sum(exchange(tiles, "x").reshape((-1, share) + tiles.shape[1:]), axis=0)
    part = spread(part.astype(jnp.bfloat16).reshape(-1, LANES), ZAX)
    part = jnp.sum(part.astype(jnp.float32), axis=0)
    part, local = lax.optimization_barrier((part, local))
    tiles = spread(part.reshape((share,) + tiles.shape[1:]), "x").reshape(tiles.shape)
    return attend(rest, their_rest, tiles, local)


def solution(mesh):
    fine = Mesh(mesh.devices.reshape(4, 2, 4, 4, 4), AXES)
    rows = P(AXES, None)
    split = P(TM, None)
    return jax.shard_map(
        body, mesh=fine, in_specs=(rows, P(), split, split, split, P()), out_specs=rows, check_vma=False
    )
```

```python
import jax
import jax.numpy as jnp
from jax import lax
from jax.experimental import pallas as pl
from jax.experimental.pallas import tpu as pltpu
from jax.sharding import Mesh
from jax.sharding import PartitionSpec as P

HEAD_WIDTH = 32
FH = 8
FW = 32
LANES = 128
BLOCK = 2 * LANES
GROUPS = 5
TILES = 24

AXES = ("y", "core", "x", "zh", "zl")
ZAX = ("zh", "zl")
TM = ("x", "zh", "zl")
PARAMS = pltpu.CompilerParams(vmem_limit_bytes=16 * 1024 * 1024)


def cost(flops, nbytes):
    return pl.CostEstimate(flops=flops, bytes_accessed=nbytes, transcendentals=0)


def exchange(blocks, axes):
    return lax.all_to_all(blocks, axes, 0, 0, tiled=True)


def spread(block, axes):
    count = lax.axis_size(axes)
    return exchange(jnp.broadcast_to(block[None], (count,) + block.shape), axes)


def norm_kernel(tokens_ref, gain_ref, out_ref):
    x = tokens_ref[...].astype(jnp.float32)
    scale = lax.rsqrt(jnp.mean(x * x, axis=1, keepdims=True) + 1e-06)
    out_ref[...] = (x * scale * gain_ref[...].astype(jnp.float32)).astype(jnp.bfloat16)


def norm(tokens, gain):
    return pl.pallas_call(
        norm_kernel,
        out_shape=jax.ShapeDtypeStruct(tokens.shape, jnp.bfloat16),
        compiler_params=PARAMS,
        cost_estimate=cost(10 * tokens.size, 4 * tokens.size),
        name="norm",
    )(tokens, gain.reshape(1, -1))


def project_kernel(mine_ref, theirs_ref, weight_ref, own_ref, other_ref):
    first = lax.axis_index("core") == 0
    for step in range(weight_ref.shape[0]):
        weight = weight_ref[step]
        for tokens_ref, out_ref in ((mine_ref, own_ref), (theirs_ref, other_ref)):
            both = jnp.dot(tokens_ref[...], weight, preferred_element_type=jnp.float32)
            for half in range(2):
                unit = 2 * step + half
                proj = both[:, half * LANES : (half + 1) * LANES]
                feat = jnp.where(proj > 0, proj, jnp.exp(jnp.minimum(proj, 0.0)) - 1.0) + 1.0
                if unit < GROUPS:
                    feat = jnp.where(first, proj, feat)
                out_ref[:, unit * LANES : (unit + 1) * LANES] = feat.astype(jnp.bfloat16)


def project(mine, theirs, weights):
    steps, depth, _ = weights.shape
    rows = mine.shape[0]
    return pl.pallas_call(
        project_kernel,
        out_shape=[jax.ShapeDtypeStruct((rows, steps * BLOCK), jnp.bfloat16)] * 2,
        compiler_params=PARAMS,
        cost_estimate=cost(4 * rows * depth * steps * BLOCK, 5 * 1024 * 1024),
        name="project",
    )(mine, theirs, weights)


def unit_of(core, mine_ref, theirs_ref, unit):
    at = slice(unit * LANES, (unit + 1) * LANES)
    return jnp.where(lax.axis_index("core") == core, mine_ref[:, at], theirs_ref[:, at])


def state_kernel(mine_ref, theirs_ref, values_ref, tiles_ref):
    lane = lax.broadcasted_iota(jnp.int32, (HEAD_WIDTH, LANES), 1) // HEAD_WIDTH
    tiles_ref[...] = jnp.zeros_like(tiles_ref)
    for g in range(GROUPS):
        values = unit_of(0, mine_ref, theirs_ref, g)
        kfeat = unit_of(1, mine_ref, theirs_ref, 2 + g)
        values_ref[:, g * LANES : (g + 1) * LANES] = values
        square = lax.dot_general(
            kfeat, values, (((0,), (0,)), ((), ())), preferred_element_type=jnp.float32
        )
        packed = jnp.zeros((HEAD_WIDTH, LANES), jnp.float32)
        for h in range(LANES // HEAD_WIDTH):
            packed = jnp.where(lane == h, square[h * HEAD_WIDTH : (h + 1) * HEAD_WIDTH], packed)
        for t in range(4):
            tiles_ref[4 * g + t] = packed[8 * t : 8 * t + 8]
        tiles_ref[4 * GROUPS, g : g + 1, :] = jnp.sum(
            kfeat.astype(jnp.float32), axis=0, keepdims=True
        )


def states(mine, theirs):
    rows = mine.shape[0]
    return pl.pallas_call(
        state_kernel,
        out_shape=(
            jax.ShapeDtypeStruct((rows, GROUPS * LANES), jnp.bfloat16),
            jax.ShapeDtypeStruct((TILES, 8, LANES), jnp.float32),
        ),
        compiler_params=PARAMS,
        cost_estimate=cost(2 * rows * GROUPS * LANES * LANES, 2 * 1024 * 1024),
        name="states",
    )(mine, theirs)


def conv_kernel(before_ref, values_ref, after_ref, weight_ref, out_ref):
    zeros = jnp.zeros((FW, LANES), jnp.float32)
    rows = FH * FW
    x = lax.broadcasted_iota(jnp.int32, (rows, LANES), 0) % FW
    weight = weight_ref[...].astype(jnp.float32)
    frames = [
        jnp.concatenate([zeros, ref[...].astype(jnp.float32), zeros], axis=0)
        for ref in (before_ref, values_ref, after_ref)
    ]
    sums = []
    for c in range(3):
        total = None
        for a in range(3):
            for b in range(3):
                tap = 9 * a + 3 * b + c
                term = frames[a][b * FW : b * FW + rows] * weight[tap : tap + 1]
                total = term if total is None else total + term
        sums.append(total)
    left = jnp.where(x == 0, 0.0, pltpu.roll(sums[0], 1, 0))
    right = jnp.where(x == FW - 1, 0.0, pltpu.roll(sums[2], rows - 1, 0))
    out_ref[...] = left + sums[1] + right


def convolve(before, values, after, weight):
    rows, width = values.shape
    block = pl.BlockSpec((rows, LANES), lambda i: (0, i))
    return pl.pallas_call(
        conv_kernel,
        grid=(width // LANES,),
        in_specs=[block, block, block, pl.BlockSpec((27, LANES), lambda i: (0, i))],
        out_specs=block,
        out_shape=jax.ShapeDtypeStruct((rows, width), jnp.float32),
        compiler_params=PARAMS,
        cost_estimate=cost(54 * rows * width, 2 * 1024 * 1024),
        name="convolve",
    )(before, values, after, weight)


def split_dot(a, b):
    high = b.astype(jnp.bfloat16)
    low = (b - high.astype(jnp.float32)).astype(jnp.bfloat16)
    return jnp.dot(a, high, preferred_element_type=jnp.float32) + jnp.dot(
        a, low, preferred_element_type=jnp.float32
    )


def attend_kernel(mine_ref, theirs_ref, tiles_ref, local_ref, out_ref):
    row = lax.broadcasted_iota(jnp.int32, (LANES, LANES), 0) // HEAD_WIDTH
    lane = lax.broadcasted_iota(jnp.int32, (LANES, LANES), 1) // HEAD_WIDTH
    same = row == lane
    for g in range(GROUPS):
        core, unit = (0, GROUPS + g) if g < 3 else (1, g - 3)
        qfeat = unit_of(core, mine_ref, theirs_ref, unit)
        packed = tiles_ref[4 * g : 4 * g + 4].reshape(HEAD_WIDTH, LANES)
        state = jnp.where(same, jnp.concatenate([packed] * 4, axis=0), 0.0)
        ksum = jnp.broadcast_to(tiles_ref[4 * GROUPS, g : g + 1, :], (LANES, LANES)).T
        ksum = jnp.where(same, ksum, 0.0)
        both = split_dot(qfeat, jnp.concatenate([state, ksum], axis=1))
        cols = slice(g * LANES, (g + 1) * LANES)
        out_ref[:, cols] = both[:, :LANES] / both[:, LANES:] + local_ref[:, cols]


def attend(mine, theirs, tiles, local):
    rows, width = local.shape
    return pl.pallas_call(
        attend_kernel,
        out_shape=jax.ShapeDtypeStruct((rows, width), jnp.float32),
        compiler_params=PARAMS,
        cost_estimate=cost(8 * rows * width * LANES, 3 * 1024 * 1024),
        name="attend",
    )(mine, theirs, tiles, local)


def swap(block):
    return lax.ppermute(block, "core", [(0, 1), (1, 0)])


def pick(w_query, w_key, w_value):
    pad = jnp.zeros((w_query.shape[0], LANES), w_query.dtype)
    cat = jnp.concatenate([w_value, w_query, w_key, pad], axis=1)
    place = 4 * lax.axis_index("core") + lax.axis_index("y")
    mine = lax.dynamic_slice_in_dim(cat, place * BLOCK, BLOCK, axis=1)
    return jnp.concatenate([mine[:, :LANES], mine[:, LANES:]], axis=0)


def body(tokens, gain, w_query, w_key, w_value, conv_weight):
    rows = w_query.shape[0]
    normed = norm(tokens, gain)
    other = swap(normed)
    column = spread(pick(w_query, w_key, w_value), ZAX)
    column = jnp.concatenate([column[:, :rows], column[:, rows:]], axis=2).reshape(-1, BLOCK)
    column, other = lax.optimization_barrier((column, other))
    weights = spread(column, ("y", "x")).reshape(lax.axis_size("y"), -1, BLOCK)

    mine, theirs = project(normed, other, weights)
    theirs = swap(theirs)
    values, tiles = states(mine, theirs)
    count = lax.axis_size(TM)
    before = lax.ppermute(values, TM, [(i, i + 1) for i in range(count - 1)])
    after = lax.ppermute(values, TM, [(i + 1, i) for i in range(count - 1)])

    share = TILES // lax.axis_size("x")
    part = jnp.sum(exchange(tiles, "x").reshape((-1, share) + tiles.shape[1:]), axis=0)
    part = part.astype(jnp.bfloat16).reshape(-1, LANES)
    part, before, after = lax.optimization_barrier((part, before, after))
    local = convolve(before, values, after, conv_weight)
    part = jnp.sum(spread(part, ZAX).astype(jnp.float32), axis=0)
    part, local = lax.optimization_barrier((part, local))
    tiles = spread(part.reshape((share,) + tiles.shape[1:]), "x").reshape(tiles.shape)
    return attend(mine, theirs, tiles, local)


def solution(mesh):
    fine = Mesh(mesh.devices.reshape(4, 2, 4, 4, 4), AXES)
    rows = P(AXES, None)
    split = P(TM, None)
    return jax.shard_map(
        body, mesh=fine, in_specs=(rows, P(), split, split, split, P()), out_specs=rows, check_vma=False
    )
```

```python
import jax
import jax.numpy as jnp
from jax import lax
from jax.experimental import pallas as pl
from jax.experimental.pallas import tpu as pltpu
from jax.sharding import Mesh
from jax.sharding import PartitionSpec as P

HEAD_WIDTH = 32
FH = 8
FW = 32
LANES = 128
BLOCK = 2 * LANES
GROUPS = 5
TILES = 24

AXES = ("y", "core", "x", "zh", "zl")
ZAX = ("zh", "zl")
TM = ("x", "zh", "zl")
PARAMS = pltpu.CompilerParams(vmem_limit_bytes=16 * 1024 * 1024)


def cost(flops, nbytes):
    return pl.CostEstimate(flops=flops, bytes_accessed=nbytes, transcendentals=0)


def exchange(blocks, axes):
    return lax.all_to_all(blocks, axes, 0, 0, tiled=True)


def spread(block, axes):
    count = lax.axis_size(axes)
    return exchange(jnp.broadcast_to(block[None], (count,) + block.shape), axes)


def norm_kernel(tokens_ref, gain_ref, out_ref):
    x = tokens_ref[...].astype(jnp.float32)
    scale = lax.rsqrt(jnp.mean(x * x, axis=1, keepdims=True) + 1e-06)
    out_ref[...] = (x * scale * gain_ref[...].astype(jnp.float32)).astype(jnp.bfloat16)


def norm(tokens, gain):
    return pl.pallas_call(
        norm_kernel,
        out_shape=jax.ShapeDtypeStruct(tokens.shape, jnp.bfloat16),
        compiler_params=PARAMS,
        cost_estimate=cost(10 * tokens.size, 4 * tokens.size),
        name="norm",
    )(tokens, gain.reshape(1, -1))


def project_kernel(mine_ref, theirs_ref, weight_ref, own_ref, other_ref):
    first = lax.axis_index("core") == 0
    for step in range(weight_ref.shape[0]):
        weight = weight_ref[step]
        for tokens_ref, out_ref in ((mine_ref, own_ref), (theirs_ref, other_ref)):
            both = jnp.dot(tokens_ref[...], weight, preferred_element_type=jnp.float32)
            for half in range(2):
                unit = 2 * step + half
                proj = both[:, half * LANES : (half + 1) * LANES]
                feat = jnp.where(proj > 0, proj, jnp.exp(jnp.minimum(proj, 0.0)) - 1.0) + 1.0
                if unit < GROUPS:
                    feat = jnp.where(first, proj, feat)
                out_ref[:, unit * LANES : (unit + 1) * LANES] = feat.astype(jnp.bfloat16)


def project(mine, theirs, weights):
    steps, depth, _ = weights.shape
    rows = mine.shape[0]
    return pl.pallas_call(
        project_kernel,
        out_shape=[jax.ShapeDtypeStruct((rows, steps * BLOCK), jnp.bfloat16)] * 2,
        compiler_params=PARAMS,
        cost_estimate=cost(4 * rows * depth * steps * BLOCK, 5 * 1024 * 1024),
        name="project",
    )(mine, theirs, weights)


def unit_of(core, mine_ref, theirs_ref, unit):
    at = slice(unit * LANES, (unit + 1) * LANES)
    return jnp.where(lax.axis_index("core") == core, mine_ref[:, at], theirs_ref[:, at])


def state_kernel(mine_ref, theirs_ref, values_ref, tiles_ref):
    lane = lax.broadcasted_iota(jnp.int32, (HEAD_WIDTH, LANES), 1) // HEAD_WIDTH
    tiles_ref[...] = jnp.zeros_like(tiles_ref)
    for g in range(GROUPS):
        values = unit_of(0, mine_ref, theirs_ref, g)
        kfeat = unit_of(1, mine_ref, theirs_ref, 2 + g)
        values_ref[:, g * LANES : (g + 1) * LANES] = values
        square = lax.dot_general(
            kfeat, values, (((0,), (0,)), ((), ())), preferred_element_type=jnp.float32
        )
        packed = jnp.zeros((HEAD_WIDTH, LANES), jnp.float32)
        for h in range(LANES // HEAD_WIDTH):
            packed = jnp.where(lane == h, square[h * HEAD_WIDTH : (h + 1) * HEAD_WIDTH], packed)
        for t in range(4):
            tiles_ref[4 * g + t] = packed[8 * t : 8 * t + 8]
        tiles_ref[4 * GROUPS, g : g + 1, :] = jnp.sum(
            kfeat.astype(jnp.float32), axis=0, keepdims=True
        )


def states(mine, theirs):
    rows = mine.shape[0]
    return pl.pallas_call(
        state_kernel,
        out_shape=(
            jax.ShapeDtypeStruct((rows, GROUPS * LANES), jnp.bfloat16),
            jax.ShapeDtypeStruct((TILES, 8, LANES), jnp.float32),
        ),
        compiler_params=PARAMS,
        cost_estimate=cost(2 * rows * GROUPS * LANES * LANES, 2 * 1024 * 1024),
        name="states",
    )(mine, theirs)


def conv_kernel(before_ref, values_ref, after_ref, weight_ref, out_ref):
    zeros = jnp.zeros((FW, LANES), jnp.float32)
    rows = FH * FW
    x = lax.broadcasted_iota(jnp.int32, (rows, LANES), 0) % FW
    weight = weight_ref[...].astype(jnp.float32)
    frames = [
        jnp.concatenate([zeros, ref[...].astype(jnp.float32), zeros], axis=0)
        for ref in (before_ref, values_ref, after_ref)
    ]
    sums = []
    for c in range(3):
        total = None
        for a in range(3):
            for b in range(3):
                tap = 9 * a + 3 * b + c
                term = frames[a][b * FW : b * FW + rows] * weight[tap : tap + 1]
                total = term if total is None else total + term
        sums.append(total)
    left = jnp.where(x == 0, 0.0, pltpu.roll(sums[0], 1, 0))
    right = jnp.where(x == FW - 1, 0.0, pltpu.roll(sums[2], rows - 1, 0))
    out_ref[...] = left + sums[1] + right


def convolve(before, values, after, weight):
    rows, width = values.shape
    block = pl.BlockSpec((rows, LANES), lambda i: (0, i))
    return pl.pallas_call(
        conv_kernel,
        grid=(width // LANES,),
        in_specs=[block, block, block, pl.BlockSpec((27, LANES), lambda i: (0, i))],
        out_specs=block,
        out_shape=jax.ShapeDtypeStruct((rows, width), jnp.float32),
        compiler_params=PARAMS,
        cost_estimate=cost(54 * rows * width, 2 * 1024 * 1024),
        name="convolve",
    )(before, values, after, weight)


def split_dot(a, b):
    high = b.astype(jnp.bfloat16)
    low = (b - high.astype(jnp.float32)).astype(jnp.bfloat16)
    return jnp.dot(a, high, preferred_element_type=jnp.float32) + jnp.dot(
        a, low, preferred_element_type=jnp.float32
    )


def attend_kernel(mine_ref, theirs_ref, tiles_ref, local_ref, out_ref):
    row = lax.broadcasted_iota(jnp.int32, (LANES, LANES), 0) // HEAD_WIDTH
    lane = lax.broadcasted_iota(jnp.int32, (LANES, LANES), 1) // HEAD_WIDTH
    same = row == lane
    for g in range(GROUPS):
        core, unit = (0, GROUPS + g) if g < 3 else (1, g - 3)
        qfeat = unit_of(core, mine_ref, theirs_ref, unit)
        packed = tiles_ref[4 * g : 4 * g + 4].reshape(HEAD_WIDTH, LANES)
        state = jnp.where(same, jnp.concatenate([packed] * 4, axis=0), 0.0)
        ksum = jnp.broadcast_to(tiles_ref[4 * GROUPS, g : g + 1, :], (LANES, LANES)).T
        ksum = jnp.where(same, ksum, 0.0)
        both = split_dot(qfeat, jnp.concatenate([state, ksum], axis=1))
        cols = slice(g * LANES, (g + 1) * LANES)
        out_ref[:, cols] = both[:, :LANES] / both[:, LANES:] + local_ref[:, cols]


def attend(mine, theirs, tiles, local):
    rows, width = local.shape
    return pl.pallas_call(
        attend_kernel,
        out_shape=jax.ShapeDtypeStruct((rows, width), jnp.float32),
        compiler_params=PARAMS,
        cost_estimate=cost(8 * rows * width * LANES, 3 * 1024 * 1024),
        name="attend",
    )(mine, theirs, tiles, local)


def swap(block):
    return lax.ppermute(block, "core", [(0, 1), (1, 0)])


def pick(w_query, w_key, w_value):
    pad = jnp.zeros((w_query.shape[0], LANES), w_query.dtype)
    cat = jnp.concatenate([w_value, w_query, w_key, pad], axis=1)
    place = 4 * lax.axis_index("core") + lax.axis_index("y")
    mine = lax.dynamic_slice_in_dim(cat, place * BLOCK, BLOCK, axis=1)
    return jnp.concatenate([mine[:, :LANES], mine[:, LANES:]], axis=0)


def body(tokens, gain, w_query, w_key, w_value, conv_weight):
    rows = w_query.shape[0]
    normed = norm(tokens, gain)
    other = swap(normed)
    column = spread(pick(w_query, w_key, w_value), ZAX)
    column = jnp.concatenate([column[:, :rows], column[:, rows:]], axis=2).reshape(-1, BLOCK)
    column, other = lax.optimization_barrier((column, other))
    weights = spread(column, ("y", "x")).reshape(lax.axis_size("y"), -1, BLOCK)

    mine, theirs = project(normed, other, weights)
    theirs = swap(theirs)
    values, tiles = states(mine, theirs)
    count = lax.axis_size(TM)
    before = lax.ppermute(values, TM, [(i, i + 1) for i in range(count - 1)])
    after = lax.ppermute(values, TM, [(i + 1, i) for i in range(count - 1)])

    share = TILES // lax.axis_size("x")
    part = jnp.sum(exchange(tiles, "x").reshape((-1, share) + tiles.shape[1:]), axis=0)
    part = part.astype(jnp.bfloat16).reshape(-1, LANES)
    local = convolve(before, values, after, conv_weight)
    part = jnp.sum(spread(part, ZAX).astype(jnp.float32), axis=0)
    part, local = lax.optimization_barrier((part, local))
    tiles = spread(part.reshape((share,) + tiles.shape[1:]), "x").reshape(tiles.shape)
    return attend(mine, theirs, tiles, local)


def solution(mesh):
    fine = Mesh(mesh.devices.reshape(4, 2, 4, 4, 4), AXES)
    rows = P(AXES, None)
    split = P(TM, None)
    return jax.shard_map(
        body, mesh=fine, in_specs=(rows, P(), split, split, split, P()), out_specs=rows, check_vma=False
    )
```

```python
import jax
import jax.numpy as jnp
from jax import lax
from jax.experimental import pallas as pl
from jax.experimental.pallas import tpu as pltpu
from jax.sharding import Mesh
from jax.sharding import PartitionSpec as P

HEAD_WIDTH = 32
FH = 8
FW = 32
LANES = 128
BLOCK = 2 * LANES
GROUPS = 5
QUARTERS = 4
TILES = 7

AXES = ("y", "core", "xh", "xl", "zh", "zl")
ZAX = ("zh", "zl")
PLANE = ("y", "xh", "xl")
TM = ("xh", "xl", "zh", "zl")
HOME = ("core", "xh", "xl")
PARAMS = pltpu.CompilerParams(vmem_limit_bytes=16 * 1024 * 1024)


def cost(flops, nbytes):
    return pl.CostEstimate(flops=flops, bytes_accessed=nbytes, transcendentals=0)


def exchange(blocks, axes):
    return lax.all_to_all(blocks, axes, 0, 0, tiled=True)


def spread(block, axes):
    count = lax.axis_size(axes)
    return exchange(jnp.broadcast_to(block[None], (count,) + block.shape), axes)


def norm_kernel(tokens_ref, gain_ref, out_ref):
    x = tokens_ref[...].astype(jnp.float32)
    scale = lax.rsqrt(jnp.mean(x * x, axis=1, keepdims=True) + 1e-06)
    out_ref[...] = (x * scale * gain_ref[...].astype(jnp.float32)).astype(jnp.bfloat16)


def norm(tokens, gain):
    return pl.pallas_call(
        norm_kernel,
        out_shape=jax.ShapeDtypeStruct(tokens.shape, jnp.bfloat16),
        compiler_params=PARAMS,
        cost_estimate=cost(10 * tokens.size, 4 * tokens.size),
        name="norm",
    )(tokens, gain.reshape(1, -1))


def project_kernel(own_ref, across_ref, other_ref, far_ref, weight_ref, *out_refs):
    lane = lax.broadcasted_iota(jnp.int32, (own_ref.shape[0], LANES), 1)
    home_ref, away_ref, keys_ref = out_refs
    for pair in range(2):
        weight = jnp.concatenate([weight_ref[2 * pair], weight_ref[2 * pair + 1]], axis=1)
        for i, tokens_ref in enumerate((own_ref, across_ref, other_ref, far_ref)):
            both = jnp.dot(tokens_ref[...], weight, preferred_element_type=jnp.float32)
            for half in range(2):
                unit = 2 * pair + half
                proj = both[:, half * LANES : (half + 1) * LANES]
                feat = jnp.where(proj > 0, proj, jnp.exp(jnp.minimum(proj, 0.0)) - 1.0) + 1.0
                if unit == 0:
                    feat = proj
                if unit == 2:
                    feat = jnp.where(lane < HEAD_WIDTH, proj, feat)
                feat = feat.astype(jnp.bfloat16)
                if unit == 3:
                    keys_ref[i] = feat
                else:
                    out = (home_ref, away_ref)[i // 2]
                    out[i % 2, :, unit * LANES : (unit + 1) * LANES] = feat


def project(own, across, other, far, weights):
    rows, depth = own.shape
    units = weights.shape[0]
    bf16 = jnp.bfloat16
    return pl.pallas_call(
        project_kernel,
        out_shape=[
            jax.ShapeDtypeStruct((2, rows, 3 * LANES), bf16),
            jax.ShapeDtypeStruct((2, rows, 3 * LANES), bf16),
            jax.ShapeDtypeStruct((4, rows, LANES), bf16),
        ],
        compiler_params=PARAMS,
        cost_estimate=cost(8 * rows * depth * units * LANES, 5 * 1024 * 1024),
        name="project",
    )(own, across, other, far, weights)


def gram(a, b):
    return lax.dot_general(a, b, (((0,), (0,)), ((), ())), preferred_element_type=jnp.float32)


def state_kernel(home_ref, away_ref, keys_ref, tiles_ref):
    first = lax.axis_index("core") == 0
    lane = lax.broadcasted_iota(jnp.int32, (HEAD_WIDTH, LANES), 1) // HEAD_WIDTH
    main, extra, sums, extra_sums = [], [], [], []
    for video, ref in enumerate((home_ref, away_ref)):
        square, corner = 0.0, 0.0
        ksum, xsum = 0.0, 0.0
        for frame in range(2):
            keys = keys_ref[2 * video + frame]
            mixed = ref[frame, :, 2 * LANES :]
            square += gram(keys, ref[frame, :, :LANES])
            corner += gram(mixed, mixed)
            ksum += jnp.sum(keys.astype(jnp.float32), axis=0, keepdims=True)
            xsum += jnp.sum(mixed.astype(jnp.float32), axis=0, keepdims=True)
        packed = jnp.zeros((HEAD_WIDTH, LANES), jnp.float32)
        for h in range(LANES // HEAD_WIDTH):
            packed = jnp.where(lane == h, square[h * HEAD_WIDTH : (h + 1) * HEAD_WIDTH], packed)
        main.append(packed)
        extra.append(corner[HEAD_WIDTH : 2 * HEAD_WIDTH])
        sums.append(ksum)
        extra_sums.append(xsum)
    zero = jnp.where(first, main[0], main[1])
    one = jnp.where(first, main[1], main[0])
    early = jnp.where(first, extra[0], extra[1])
    late = pltpu.roll(jnp.where(first, extra[1], extra[0]), HEAD_WIDTH, 1)
    corner = jnp.where(lane == 0, early, jnp.where(lane == 1, late, 0.0))
    for half in range(2):
        for i, block in enumerate((zero, one, corner)):
            for t in range(2):
                at = 8 * (2 * half + t)
                tiles_ref[half, 2 * i + t] = block[at : at + 8]
        tiles_ref[half, 6] = jnp.zeros((8, LANES), jnp.float32)
        tiles_ref[half, 6, 0:1, :] = jnp.where(first, sums[0], sums[1])
        tiles_ref[half, 6, 1:2, :] = jnp.where(first, sums[1], sums[0])
        tiles_ref[half, 6, 2:3, :] = jnp.where(first, extra_sums[0], extra_sums[1])
        tiles_ref[half, 6, 3:4, :] = jnp.where(first, extra_sums[1], extra_sums[0])


def states(home, away, keys):
    return pl.pallas_call(
        state_kernel,
        out_shape=jax.ShapeDtypeStruct((2, TILES, 8, LANES), jnp.float32),
        compiler_params=PARAMS,
        cost_estimate=cost(16 * home.shape[1] * LANES * LANES, 2 * 1024 * 1024),
        name="states",
    )(home, away, keys)


def quarter_of(q, refs):
    core = lax.axis_index("core") != q // 2
    side = lax.axis_index("xl") != q % 2

    def pick_one(unit):
        at = slice(unit * LANES, (unit + 1) * LANES)
        own, across, other, far = (ref[0, :, at] for ref in refs)
        return jnp.where(core, jnp.where(side, far, other), jnp.where(side, across, own))

    return pick_one


def assemble_kernel(own_ref, across_ref, other_ref, far_ref, values_ref, query_ref):
    refs = (own_ref, across_ref, other_ref, far_ref)
    lane = lax.broadcasted_iota(jnp.int32, (own_ref.shape[1], LANES), 1) // HEAD_WIDTH
    value, query = 0.0, 0.0
    for q in range(QUARTERS):
        take = quarter_of(q, refs)
        values_ref[:, q * LANES : (q + 1) * LANES] = take(0)
        query_ref[:, q * LANES : (q + 1) * LANES] = take(1)
        mixed = take(2).astype(jnp.float32)
        moved = pltpu.roll(mixed, q * HEAD_WIDTH, 1) if q else mixed
        value = jnp.where(lane == q, moved, value)
        shift = (q - 2) % 4 * HEAD_WIDTH
        moved = pltpu.roll(mixed, shift, 1) if shift else mixed
        query = jnp.where(lane == q, moved, query)
    values_ref[:, QUARTERS * LANES :] = value.astype(jnp.bfloat16)
    query_ref[:, QUARTERS * LANES :] = query.astype(jnp.bfloat16)


def assemble(own, across, other, far):
    rows = own.shape[1]
    return pl.pallas_call(
        assemble_kernel,
        out_shape=[jax.ShapeDtypeStruct((rows, GROUPS * LANES), jnp.bfloat16)] * 2,
        compiler_params=PARAMS,
        cost_estimate=cost(rows * 4 * LANES, 2 * 1024 * 1024),
        name="assemble",
    )(own, across, other, far)


def conv_kernel(before_ref, values_ref, after_ref, weight_ref, out_ref):
    zeros = jnp.zeros((FW, LANES), jnp.float32)
    rows = FH * FW
    x = lax.broadcasted_iota(jnp.int32, (rows, LANES), 0) % FW
    weight = weight_ref[...].astype(jnp.float32)
    frames = [
        jnp.concatenate([zeros, ref[...].astype(jnp.float32), zeros], axis=0)
        for ref in (before_ref, values_ref, after_ref)
    ]
    sums = []
    for c in range(3):
        total = None
        for a in range(3):
            for b in range(3):
                tap = 9 * a + 3 * b + c
                term = frames[a][b * FW : b * FW + rows] * weight[tap : tap + 1]
                total = term if total is None else total + term
        sums.append(total)
    left = jnp.where(x == 0, 0.0, pltpu.roll(sums[0], 1, 0))
    right = jnp.where(x == FW - 1, 0.0, pltpu.roll(sums[2], rows - 1, 0))
    out_ref[...] = left + sums[1] + right


def convolve(before, values, after, weight):
    rows, width = values.shape
    block = pl.BlockSpec((rows, LANES), lambda i: (0, i))
    return pl.pallas_call(
        conv_kernel,
        grid=(width // LANES,),
        in_specs=[block, block, block, pl.BlockSpec((27, LANES), lambda i: (0, i))],
        out_specs=block,
        out_shape=jax.ShapeDtypeStruct((rows, width), jnp.float32),
        compiler_params=PARAMS,
        cost_estimate=cost(54 * rows * width, 2 * 1024 * 1024),
        name="convolve",
    )(before, values, after, weight)


def split_dot(a, b):
    high = b.astype(jnp.bfloat16)
    low = (b - high.astype(jnp.float32)).astype(jnp.bfloat16)
    return jnp.dot(a, high, preferred_element_type=jnp.float32) + jnp.dot(
        a, low, preferred_element_type=jnp.float32
    )


def attend_kernel(query_ref, tiles_ref, local_ref, out_ref):
    first = lax.axis_index("core") == 0
    row = lax.broadcasted_iota(jnp.int32, (LANES, LANES), 0) // HEAD_WIDTH
    lane = lax.broadcasted_iota(jnp.int32, (LANES, LANES), 1) // HEAD_WIDTH
    same = row == lane
    packs, sums = [], []
    extra, extra_sum = 0.0, 0.0
    for q in range(QUARTERS):
        low, high = (q // 2 * 4 + half * 2 + q % 2 for half in range(2))
        parts = [
            jnp.where(first, tiles_ref[at, t], tiles_ref[at, 2 + t])
            for at in (low, high)
            for t in range(2)
        ]
        packs.append(jnp.concatenate(parts, axis=0))
        ksum = tiles_ref[low, 6]
        sums.append(jnp.where(first, ksum[0:1], ksum[1:2]))
        corner = jnp.concatenate([tiles_ref[at, 4 + t] for at in (low, high) for t in range(2)], 0)
        corner = jnp.where(first, corner, pltpu.roll(corner, LANES - HEAD_WIDTH, 1))
        corner = pltpu.roll(corner, q * HEAD_WIDTH, 1) if q else corner
        extra = jnp.where(lane[:HEAD_WIDTH] == q, corner, extra)
        shift = (q - 1) % 4 * HEAD_WIDTH
        xsum = pltpu.roll(ksum, shift, 1) if shift else ksum
        xsum = jnp.where(first, xsum[2:3], xsum[3:4])
        extra_sum = jnp.where(lane[:1] == q, xsum, extra_sum)
    packs.append(extra)
    sums.append(extra_sum)
    for g in range(GROUPS):
        cols = slice(g * LANES, (g + 1) * LANES)
        state = jnp.where(same, jnp.concatenate([packs[g]] * 4, axis=0), 0.0)
        ksum = jnp.where(same, jnp.broadcast_to(sums[g], (LANES, LANES)).T, 0.0)
        both = split_dot(query_ref[:, cols], jnp.concatenate([state, ksum], axis=1))
        out_ref[:, cols] = both[:, :LANES] / both[:, LANES:] + local_ref[:, cols]


def attend(query, tiles, local):
    rows, width = local.shape
    return pl.pallas_call(
        attend_kernel,
        out_shape=jax.ShapeDtypeStruct((rows, width), jnp.float32),
        compiler_params=PARAMS,
        cost_estimate=cost(8 * rows * width * LANES, 3 * 1024 * 1024),
        name="attend",
    )(query, tiles, local)


def pick_kernel(cat_ref, out_ref):
    y, core = lax.axis_index("y"), lax.axis_index("core")
    width = GROUPS * LANES
    row = lax.broadcasted_iota(jnp.int32, (LANES, LANES), 0)
    lane = lax.broadcasted_iota(jnp.int32, (LANES, LANES), 1)
    blocks = []
    for t in range(2):
        quarter = 2 * core + t
        whole, mixed = [], 0.0
        for i in range(3):
            at = i * width + t * LANES
            left, right = cat_ref[:, at : at + LANES], cat_ref[:, at + BLOCK : at + BLOCK + LANES]
            whole.append(jnp.where(core == 0, left, right).astype(jnp.float32))
            place = (0, 2, 1)[i] * HEAD_WIDTH
            take = jnp.logical_and(lane >= place, lane < place + HEAD_WIDTH)
            take = jnp.logical_and(take, row == quarter * HEAD_WIDTH + lane - place)
            take = jnp.where(take, 1.0, 0.0).astype(jnp.bfloat16)
            tail = cat_ref[:, i * width + 2 * BLOCK : (i + 1) * width]
            mixed += jnp.dot(tail, take, preferred_element_type=jnp.float32)
        value, query, key = whole
        block = jnp.where(y == 1, query, jnp.where(y == 2, mixed, key))
        blocks.append(jnp.where(y == 0, value, block))
    block = jnp.concatenate(blocks, axis=0).astype(jnp.bfloat16)
    for i in range(out_ref.shape[0]):
        out_ref[i] = block


def pick(w_query, w_key, w_value, copies):
    rows = w_query.shape[0]
    return pl.pallas_call(
        pick_kernel,
        out_shape=jax.ShapeDtypeStruct((copies, 2 * rows, LANES), jnp.bfloat16),
        compiler_params=PARAMS,
        cost_estimate=cost(0, 4 * 1024 * rows),
        name="pick",
    )(jnp.concatenate([w_value, w_query, w_key], axis=1))


def flip(block, axis):
    return lax.ppermute(block, axis, [(0, 1), (1, 0)])


def body(tokens, gain, w_query, w_key, w_value, conv_weight):
    rows = w_query.shape[0]
    own = norm(tokens, gain)
    across, other = flip(own, "xl"), flip(own, "core")
    column = exchange(pick(w_query, w_key, w_value, lax.axis_size(ZAX)), ZAX)
    column = column.reshape(-1, 2, rows, LANES).transpose(1, 0, 2, 3).reshape(2, -1, LANES)
    column, across, other = lax.optimization_barrier((column, across, other))
    far = flip(across, "core")
    weights = exchange(
        jnp.broadcast_to(column[None], (8,) + column.shape).reshape((-1,) + column.shape[1:]), PLANE
    )
    weights = weights.reshape(lax.axis_size("y"), -1, LANES)

    home, away, keys = project(own, across, other, far, weights)
    tiles = states(home, away, keys)
    back = flip(away, "core")
    values, query = assemble(home, flip(home[1:], "xl"), back, flip(back[1:], "xl"))
    count = lax.axis_size(TM)
    before = lax.ppermute(values, TM, [(i, i + 1) for i in range(count - 1)])
    after = lax.ppermute(values, TM, [(i + 1, i) for i in range(count - 1)])

    part = jnp.sum(exchange(tiles, "xh"), axis=0)
    part = part.astype(jnp.bfloat16).reshape(-1, LANES)
    part = jnp.sum(spread(part, ZAX).astype(jnp.float32), axis=0)
    part, before, after = lax.optimization_barrier((part, before, after))
    local = convolve(before, values, after, conv_weight)
    tiles = spread(part.reshape(tiles.shape[1:]), HOME)
    return attend(query, tiles, local)


def solution(mesh):
    fine = Mesh(mesh.devices.reshape(4, 2, 2, 2, 4, 4), AXES)
    rows = P(AXES, None)
    split = P(TM, None)
    return jax.shard_map(
        body, mesh=fine, in_specs=(rows, P(), split, split, split, P()), out_specs=rows, check_vma=False
    )
```

```python
import jax
import jax.numpy as jnp
from jax import lax
from jax.experimental import pallas as pl
from jax.experimental.pallas import tpu as pltpu
from jax.sharding import Mesh
from jax.sharding import PartitionSpec as P

HEAD_WIDTH = 32
FH = 8
FW = 32
LANES = 128
BLOCK = 2 * LANES
GROUPS = 5
TILES = 24

AXES = ("y", "core", "x", "zh", "zl")
ZAX = ("zh", "zl")
TM = ("x", "zh", "zl")
NEAR = ("x", "zl")
PARAMS = pltpu.CompilerParams(vmem_limit_bytes=16 * 1024 * 1024)


def cost(flops, nbytes):
    return pl.CostEstimate(flops=flops, bytes_accessed=nbytes, transcendentals=0)


def exchange(blocks, axes):
    return lax.all_to_all(blocks, axes, 0, 0, tiled=True)


def spread(block, axes):
    count = lax.axis_size(axes)
    return exchange(jnp.broadcast_to(block[None], (count,) + block.shape), axes)


def norm_kernel(tokens_ref, gain_ref, out_ref):
    x = tokens_ref[...].astype(jnp.float32)
    scale = lax.rsqrt(jnp.mean(x * x, axis=1, keepdims=True) + 1e-06)
    out_ref[...] = (x * scale * gain_ref[...].astype(jnp.float32)[None]).astype(jnp.bfloat16)


def norm(tokens, gain):
    return pl.pallas_call(
        norm_kernel,
        out_shape=jax.ShapeDtypeStruct(tokens.shape, jnp.bfloat16),
        compiler_params=PARAMS,
        cost_estimate=cost(10 * tokens.size, 4 * tokens.size),
        name="norm",
    )(tokens, gain)


def project_kernel(tokens_ref, weight_ref, out_ref):
    first = lax.axis_index("core") == 0
    for step in range(4):
        places = [jnp.where(first, 4 * step + x, 4 * x + step) for x in range(4)]
        weight = jnp.concatenate([weight_ref[place] for place in places], axis=0)
        both = jnp.dot(tokens_ref[...], weight, preferred_element_type=jnp.float32)
        for half in range(2):
            unit = 2 * step + half
            proj = both[:, half * LANES : (half + 1) * LANES]
            feat = jnp.where(proj > 0, proj, jnp.exp(jnp.minimum(proj, 0.0)) - 1.0) + 1.0
            if unit < GROUPS:
                feat = jnp.where(first, proj, feat)
            out_ref[:, unit * LANES : (unit + 1) * LANES] = feat.astype(jnp.bfloat16)


def project(tokens, weights):
    rows, depth = tokens.shape
    steps = 4
    return pl.pallas_call(
        project_kernel,
        out_shape=jax.ShapeDtypeStruct((rows, steps * BLOCK), jnp.bfloat16),
        compiler_params=PARAMS,
        cost_estimate=cost(2 * rows * depth * steps * BLOCK, 4 * 1024 * 1024),
        name="project",
    )(tokens, weights)


def unit_of(core, mine_ref, theirs_ref, unit):
    at = slice(unit * LANES, (unit + 1) * LANES)
    return jnp.where(lax.axis_index("core") == core, mine_ref[:, at], theirs_ref[:, at])


def state_kernel(mine_ref, theirs_ref, values_ref, tiles_ref):
    lane = lax.broadcasted_iota(jnp.int32, (HEAD_WIDTH, LANES), 1) // HEAD_WIDTH
    tiles_ref[...] = jnp.zeros_like(tiles_ref)
    for g in range(GROUPS):
        values = unit_of(0, mine_ref, theirs_ref, g)
        kfeat = unit_of(1, mine_ref, theirs_ref, 2 + g)
        values_ref[:, g * LANES : (g + 1) * LANES] = values
        square = lax.dot_general(
            kfeat, values, (((0,), (0,)), ((), ())), preferred_element_type=jnp.float32
        )
        packed = jnp.zeros((HEAD_WIDTH, LANES), jnp.float32)
        for h in range(LANES // HEAD_WIDTH):
            packed = jnp.where(lane == h, square[h * HEAD_WIDTH : (h + 1) * HEAD_WIDTH], packed)
        for t in range(4):
            tiles_ref[4 * g + t] = packed[8 * t : 8 * t + 8]
        tiles_ref[4 * GROUPS, g : g + 1, :] = jnp.sum(
            kfeat.astype(jnp.float32), axis=0, keepdims=True
        )


def states(mine, theirs):
    rows = mine.shape[0]
    return pl.pallas_call(
        state_kernel,
        out_shape=(
            jax.ShapeDtypeStruct((rows, GROUPS * LANES), jnp.bfloat16),
            jax.ShapeDtypeStruct((TILES, 8, LANES), jnp.float32),
        ),
        compiler_params=PARAMS,
        cost_estimate=cost(2 * rows * GROUPS * LANES * LANES, 2 * 1024 * 1024),
        name="states",
    )(mine, theirs)


def conv_kernel(before_ref, values_ref, after_ref, weight_ref, out_ref):
    zeros = jnp.zeros((FW, LANES), jnp.float32)
    rows = FH * FW
    x = lax.broadcasted_iota(jnp.int32, (rows, LANES), 0) % FW
    weight = weight_ref[...].astype(jnp.float32)
    frames = [
        jnp.concatenate([zeros, ref[...].astype(jnp.float32), zeros], axis=0)
        for ref in (before_ref, values_ref, after_ref)
    ]
    sums = []
    for c in range(3):
        total = None
        for a in range(3):
            for b in range(3):
                tap = 9 * a + 3 * b + c
                term = frames[a][b * FW : b * FW + rows] * weight[tap : tap + 1]
                total = term if total is None else total + term
        sums.append(total)
    left = jnp.where(x == 0, 0.0, pltpu.roll(sums[0], 1, 0))
    right = jnp.where(x == FW - 1, 0.0, pltpu.roll(sums[2], rows - 1, 0))
    out_ref[...] = left + sums[1] + right


def convolve(before, values, after, weight):
    rows, width = values.shape
    block = pl.BlockSpec((rows, LANES), lambda i: (0, i))
    return pl.pallas_call(
        conv_kernel,
        grid=(width // LANES,),
        in_specs=[block, block, block, pl.BlockSpec((27, LANES), lambda i: (0, i))],
        out_specs=block,
        out_shape=jax.ShapeDtypeStruct((rows, width), jnp.float32),
        compiler_params=PARAMS,
        cost_estimate=cost(54 * rows * width, 2 * 1024 * 1024),
        name="convolve",
    )(before, values, after, weight)


def split_dot(a, b):
    high = b.astype(jnp.bfloat16)
    low = (b - high.astype(jnp.float32)).astype(jnp.bfloat16)
    return jnp.dot(
        jnp.concatenate([a, a], axis=1),
        jnp.concatenate([high, low], axis=0),
        preferred_element_type=jnp.float32,
    )


def attend_kernel(mine_ref, theirs_ref, tiles_ref, local_ref, out_ref):
    row = lax.broadcasted_iota(jnp.int32, (LANES, LANES), 0) // HEAD_WIDTH
    lane = lax.broadcasted_iota(jnp.int32, (LANES, LANES), 1) // HEAD_WIDTH
    same = row == lane
    for g in range(GROUPS):
        core, unit = (0, GROUPS + g) if g < 3 else (1, g - 3)
        qfeat = unit_of(core, mine_ref, theirs_ref, unit)
        packed = tiles_ref[4 * g : 4 * g + 4].reshape(HEAD_WIDTH, LANES)
        state = jnp.where(same, jnp.concatenate([packed] * 4, axis=0), 0.0)
        ksum = jnp.broadcast_to(tiles_ref[4 * GROUPS, g : g + 1, :], (LANES, LANES)).T
        ksum = jnp.where(same, ksum, 0.0)
        both = split_dot(qfeat, jnp.concatenate([state, ksum], axis=1))
        cols = slice(g * LANES, (g + 1) * LANES)
        out_ref[:, cols] = both[:, :LANES] / both[:, LANES:] + local_ref[:, cols]


def attend(mine, theirs, tiles, local):
    rows, width = local.shape
    return pl.pallas_call(
        attend_kernel,
        out_shape=jax.ShapeDtypeStruct((rows, width), jnp.float32),
        compiler_params=PARAMS,
        cost_estimate=cost(8 * rows * width * LANES, 3 * 1024 * 1024),
        name="attend",
    )(mine, theirs, tiles, local)


def spread_crossed(block, turn):
    ys, xs = lax.axis_size("y"), lax.axis_size("x")
    place = lambda core, y, x: (core * ys + y) * xs + x
    along_x = [[place(turn, y, x) for x in range(xs)] for y in range(ys)]
    along_y = [[place(1 - turn, y, x) for y in range(ys)] for x in range(xs)]
    blocks = jnp.broadcast_to(block[None], (xs,) + block.shape)
    return lax.all_to_all(
        blocks, ("core", "y", "x"), 0, 0, tiled=True, axis_index_groups=along_x + along_y
    )


def swap(block):
    return lax.ppermute(block, "core", [(0, 1), (1, 0)])


def pick(w_query, w_key, w_value):
    pad = jnp.zeros((w_query.shape[0], LANES), w_query.dtype)
    cat = jnp.concatenate([w_value, w_query, w_key, pad], axis=1)
    place = 4 * lax.axis_index("core") + lax.axis_index("y")
    mine = lax.dynamic_slice_in_dim(cat, place * BLOCK, BLOCK, axis=1)
    return jnp.concatenate([mine[:, :LANES], mine[:, LANES:]], axis=0)


def body(tokens, gain, w_query, w_key, w_value, conv_weight):
    rows = w_query.shape[0]
    normed = norm(tokens, gain)
    other = swap(normed)
    column = spread(pick(w_query, w_key, w_value), ZAX)
    column = jnp.concatenate([column[:, :rows], column[:, rows:]], axis=2).reshape(-1, BLOCK)
    column, other = lax.optimization_barrier((column, other))
    weights = spread_crossed(spread_crossed(column, 0).reshape(-1, BLOCK), 1)
    weights = weights.reshape((-1,) + column.shape)

    theirs = swap(project(other, weights))
    mine = project(normed, weights)
    values, tiles = states(mine, theirs)
    count = lax.axis_size(TM)
    before = lax.ppermute(values, TM, [(i, i + 1) for i in range(count - 1)])
    after = lax.ppermute(values, TM, [(i + 1, i) for i in range(count - 1)])

    share = TILES // lax.axis_size(NEAR)
    part = jnp.sum(exchange(tiles, NEAR).reshape((-1, share) + tiles.shape[1:]), axis=0)
    part = part.astype(jnp.bfloat16).reshape(-1, LANES)
    part = jnp.sum(spread(part, "zh").astype(jnp.float32), axis=0)
    local = convolve(before, values, after, conv_weight)
    part, local = lax.optimization_barrier((part, local))
    tiles = spread(part.reshape((share,) + tiles.shape[1:]), NEAR).reshape(tiles.shape)
    return attend(mine, theirs, tiles, local)


def solution(mesh):
    fine = Mesh(mesh.devices.reshape(4, 2, 4, 8, 2), AXES)
    rows = P(AXES, None)
    split = P(TM, None)
    return jax.shard_map(
        body, mesh=fine, in_specs=(rows, P(), split, split, split, P()), out_specs=rows, check_vma=False
    )
```

```python
import jax
import jax.numpy as jnp
from jax import lax
from jax.experimental import pallas as pl
from jax.experimental.pallas import tpu as pltpu
from jax.sharding import Mesh
from jax.sharding import PartitionSpec as P

HEAD_WIDTH = 32
FH = 8
FW = 32
LANES = 128
BLOCK = 2 * LANES
GROUPS = 5
TILES = 24

AXES = ("y", "core", "x", "zh", "zl")
ZAX = ("zh", "zl")
TM = ("x", "zh", "zl")
NEAR = ("x", "zl")
PARAMS = pltpu.CompilerParams(vmem_limit_bytes=16 * 1024 * 1024)


def cost(flops, nbytes):
    return pl.CostEstimate(flops=flops, bytes_accessed=nbytes, transcendentals=0)


def exchange(blocks, axes):
    return lax.all_to_all(blocks, axes, 0, 0, tiled=True)


def spread(block, axes):
    count = lax.axis_size(axes)
    return exchange(jnp.broadcast_to(block[None], (count,) + block.shape), axes)


def norm_kernel(tokens_ref, gain_ref, out_ref):
    x = tokens_ref[...].astype(jnp.float32)
    scale = lax.rsqrt(jnp.mean(x * x, axis=1, keepdims=True) + 1e-06)
    out_ref[...] = (x * scale * gain_ref[...].astype(jnp.float32)[None]).astype(jnp.bfloat16)


def norm(tokens, gain):
    return pl.pallas_call(
        norm_kernel,
        out_shape=jax.ShapeDtypeStruct(tokens.shape, jnp.bfloat16),
        compiler_params=PARAMS,
        cost_estimate=cost(10 * tokens.size, 4 * tokens.size),
        name="norm",
    )(tokens, gain)


def project_kernel(tokens_ref, weight_ref, out_ref):
    first = lax.axis_index("core") == 0
    for step in range(4):
        places = [jnp.where(first, 4 * step + x, 4 * x + step) for x in range(4)]
        weight = jnp.concatenate([weight_ref[place] for place in places], axis=0)
        both = jnp.dot(tokens_ref[...], weight, preferred_element_type=jnp.float32)
        for half in range(2):
            unit = 2 * step + half
            proj = both[:, half * LANES : (half + 1) * LANES]
            feat = jnp.where(proj > 0, proj, jnp.exp(jnp.minimum(proj, 0.0)) - 1.0) + 1.0
            if unit < GROUPS:
                feat = jnp.where(first, proj, feat)
            out_ref[:, unit * LANES : (unit + 1) * LANES] = feat.astype(jnp.bfloat16)


def project(tokens, weights):
    rows, depth = tokens.shape
    steps = 4
    return pl.pallas_call(
        project_kernel,
        out_shape=jax.ShapeDtypeStruct((rows, steps * BLOCK), jnp.bfloat16),
        compiler_params=PARAMS,
        cost_estimate=cost(2 * rows * depth * steps * BLOCK, 4 * 1024 * 1024),
        name="project",
    )(tokens, weights)


def unit_of(core, mine_ref, theirs_ref, unit):
    at = slice(unit * LANES, (unit + 1) * LANES)
    return jnp.where(lax.axis_index("core") == core, mine_ref[:, at], theirs_ref[:, at])


def state_kernel(mine_ref, theirs_ref, values_ref, tiles_ref):
    lane = lax.broadcasted_iota(jnp.int32, (HEAD_WIDTH, LANES), 1) // HEAD_WIDTH
    tiles_ref[...] = jnp.zeros_like(tiles_ref)
    for g in range(GROUPS):
        values = unit_of(0, mine_ref, theirs_ref, g)
        kfeat = unit_of(1, mine_ref, theirs_ref, 2 + g)
        values_ref[:, g * LANES : (g + 1) * LANES] = values
        square = lax.dot_general(
            kfeat, values, (((0,), (0,)), ((), ())), preferred_element_type=jnp.float32
        )
        packed = jnp.zeros((HEAD_WIDTH, LANES), jnp.float32)
        for h in range(LANES // HEAD_WIDTH):
            packed = jnp.where(lane == h, square[h * HEAD_WIDTH : (h + 1) * HEAD_WIDTH], packed)
        for t in range(4):
            tiles_ref[4 * g + t] = packed[8 * t : 8 * t + 8]
        tiles_ref[4 * GROUPS, g : g + 1, :] = jnp.sum(
            kfeat.astype(jnp.float32), axis=0, keepdims=True
        )


def states(mine, theirs):
    rows = mine.shape[0]
    return pl.pallas_call(
        state_kernel,
        out_shape=(
            jax.ShapeDtypeStruct((rows, GROUPS * LANES), jnp.bfloat16),
            jax.ShapeDtypeStruct((TILES, 8, LANES), jnp.float32),
        ),
        compiler_params=PARAMS,
        cost_estimate=cost(2 * rows * GROUPS * LANES * LANES, 2 * 1024 * 1024),
        name="states",
    )(mine, theirs)


def conv_kernel(before_ref, values_ref, after_ref, weight_ref, out_ref):
    zeros = jnp.zeros((FW, LANES), jnp.float32)
    rows = FH * FW
    x = lax.broadcasted_iota(jnp.int32, (rows, LANES), 0) % FW
    weight = weight_ref[...].astype(jnp.float32)
    frames = [
        jnp.concatenate([zeros, ref[...].astype(jnp.float32), zeros], axis=0)
        for ref in (before_ref, values_ref, after_ref)
    ]
    sums = []
    for c in range(3):
        total = None
        for a in range(3):
            for b in range(3):
                tap = 9 * a + 3 * b + c
                term = frames[a][b * FW : b * FW + rows] * weight[tap : tap + 1]
                total = term if total is None else total + term
        sums.append(total)
    left = jnp.where(x == 0, 0.0, pltpu.roll(sums[0], 1, 0))
    right = jnp.where(x == FW - 1, 0.0, pltpu.roll(sums[2], rows - 1, 0))
    out_ref[...] = left + sums[1] + right


def convolve(before, values, after, weight):
    rows, width = values.shape
    block = pl.BlockSpec((rows, LANES), lambda i: (0, i))
    return pl.pallas_call(
        conv_kernel,
        grid=(width // LANES,),
        in_specs=[block, block, block, pl.BlockSpec((27, LANES), lambda i: (0, i))],
        out_specs=block,
        out_shape=jax.ShapeDtypeStruct((rows, width), jnp.float32),
        compiler_params=PARAMS,
        cost_estimate=cost(54 * rows * width, 2 * 1024 * 1024),
        name="convolve",
    )(before, values, after, weight)


def split_dot(a, b):
    high = b.astype(jnp.bfloat16)
    low = (b - high.astype(jnp.float32)).astype(jnp.bfloat16)
    return jnp.dot(
        jnp.concatenate([a, a], axis=1),
        jnp.concatenate([high, low], axis=0),
        preferred_element_type=jnp.float32,
    )


def attend_kernel(mine_ref, theirs_ref, tiles_ref, local_ref, out_ref):
    row = lax.broadcasted_iota(jnp.int32, (LANES, LANES), 0) // HEAD_WIDTH
    lane = lax.broadcasted_iota(jnp.int32, (LANES, LANES), 1) // HEAD_WIDTH
    same = row == lane
    for g in range(GROUPS):
        core, unit = (0, GROUPS + g) if g < 3 else (1, g - 3)
        qfeat = unit_of(core, mine_ref, theirs_ref, unit)
        packed = tiles_ref[4 * g : 4 * g + 4].reshape(HEAD_WIDTH, LANES)
        state = jnp.where(same, jnp.concatenate([packed] * 4, axis=0), 0.0)
        ksum = jnp.broadcast_to(tiles_ref[4 * GROUPS, g : g + 1, :], (LANES, LANES)).T
        ksum = jnp.where(same, ksum, 0.0)
        both = split_dot(qfeat, jnp.concatenate([state, ksum], axis=1))
        cols = slice(g * LANES, (g + 1) * LANES)
        out_ref[:, cols] = both[:, :LANES] / both[:, LANES:] + local_ref[:, cols]


def attend(mine, theirs, tiles, local):
    rows, width = local.shape
    return pl.pallas_call(
        attend_kernel,
        out_shape=jax.ShapeDtypeStruct((rows, width), jnp.float32),
        compiler_params=PARAMS,
        cost_estimate=cost(8 * rows * width * LANES, 3 * 1024 * 1024),
        name="attend",
    )(mine, theirs, tiles, local)


def spread_crossed(block, turn):
    ys, xs = lax.axis_size("y"), lax.axis_size("x")
    place = lambda core, y, x: (core * ys + y) * xs + x
    along_x = [[place(turn, y, x) for x in range(xs)] for y in range(ys)]
    along_y = [[place(1 - turn, y, x) for y in range(ys)] for x in range(xs)]
    blocks = jnp.broadcast_to(block[None], (xs,) + block.shape)
    return lax.all_to_all(
        blocks, ("core", "y", "x"), 0, 0, tiled=True, axis_index_groups=along_x + along_y
    )


def swap(block):
    return lax.ppermute(block, "core", [(0, 1), (1, 0)])


def pick(w_query, w_key, w_value):
    pad = jnp.zeros((w_query.shape[0], LANES), w_query.dtype)
    cat = jnp.concatenate([w_value, w_query, w_key, pad], axis=1)
    place = 4 * lax.axis_index("core") + lax.axis_index("y")
    mine = lax.dynamic_slice_in_dim(cat, place * BLOCK, BLOCK, axis=1)
    return jnp.concatenate([mine[:, :LANES], mine[:, LANES:]], axis=0)


def body(tokens, gain, w_query, w_key, w_value, conv_weight):
    rows = w_query.shape[0]
    normed = norm(tokens, gain)
    other = swap(normed)
    column = spread(pick(w_query, w_key, w_value), ZAX)
    column = jnp.concatenate([column[:, :rows], column[:, rows:]], axis=2).reshape(-1, BLOCK)
    column, other = lax.optimization_barrier((column, other))
    weights = spread_crossed(spread_crossed(column, 0).reshape(-1, BLOCK), 1)
    weights = weights.reshape((-1,) + column.shape)

    theirs = swap(project(other, weights))
    mine = project(normed, weights)
    values, tiles = states(mine, theirs)
    count = lax.axis_size(TM)
    before = lax.ppermute(values, TM, [(i, i + 1) for i in range(count - 1)])
    after = lax.ppermute(values, TM, [(i + 1, i) for i in range(count - 1)])

    share = TILES // lax.axis_size(NEAR)
    part = jnp.sum(exchange(tiles, NEAR).reshape((-1, share) + tiles.shape[1:]), axis=0)
    part = part.astype(jnp.bfloat16).reshape(-1, LANES)
    part = spread(part, ZAX).astype(jnp.float32)
    part = jnp.sum(part.reshape((lax.axis_size("zh"), -1) + part.shape[1:]), axis=0)
    part, before, after = lax.optimization_barrier((part, before, after))
    local = convolve(before, values, after, conv_weight)
    tiles = spread(part.reshape((-1,) + tiles.shape[1:]), "x").reshape(tiles.shape)
    return attend(mine, theirs, tiles, local)


def solution(mesh):
    fine = Mesh(mesh.devices.reshape(4, 2, 4, 8, 2), AXES)
    rows = P(AXES, None)
    split = P(TM, None)
    return jax.shard_map(
        body, mesh=fine, in_specs=(rows, P(), split, split, split, P()), out_specs=rows, check_vma=False
    )
```

```python
import jax
import jax.numpy as jnp
from jax import lax
from jax.experimental import pallas as pl
from jax.experimental.pallas import tpu as pltpu
from jax.sharding import Mesh
from jax.sharding import PartitionSpec as P

HEAD_WIDTH = 32
FH = 8
FW = 32
LANES = 128
BLOCK = 2 * LANES
GROUPS = 5
TILES = 24

AXES = ("y", "core", "x", "zh", "zl")
ZAX = ("zh", "zl")
TM = ("x", "zh", "zl")
NEAR = ("x", "zl")
PARAMS = pltpu.CompilerParams(vmem_limit_bytes=16 * 1024 * 1024)


def cost(flops, nbytes):
    return pl.CostEstimate(flops=flops, bytes_accessed=nbytes, transcendentals=0)


def exchange(blocks, axes):
    return lax.all_to_all(blocks, axes, 0, 0, tiled=True)


def spread(block, axes):
    count = lax.axis_size(axes)
    return exchange(jnp.broadcast_to(block[None], (count,) + block.shape), axes)


def norm_kernel(tokens_ref, gain_ref, out_ref):
    x = tokens_ref[...].astype(jnp.float32)
    scale = lax.rsqrt(jnp.mean(x * x, axis=1, keepdims=True) + 1e-06)
    out_ref[...] = (x * scale * gain_ref[...].astype(jnp.float32)[None]).astype(jnp.bfloat16)


def norm(tokens, gain):
    return pl.pallas_call(
        norm_kernel,
        out_shape=jax.ShapeDtypeStruct(tokens.shape, jnp.bfloat16),
        compiler_params=PARAMS,
        cost_estimate=cost(10 * tokens.size, 4 * tokens.size),
        name="norm",
    )(tokens, gain)


def project_kernel(tokens_ref, weight_ref, out_ref):
    first = lax.axis_index("core") == 0
    for step in range(4):
        places = [jnp.where(first, 4 * step + x, 4 * x + step) for x in range(4)]
        weight = jnp.concatenate([weight_ref[place] for place in places], axis=0)
        both = jnp.dot(tokens_ref[...], weight, preferred_element_type=jnp.float32)
        for half in range(2):
            unit = 2 * step + half
            proj = both[:, half * LANES : (half + 1) * LANES]
            feat = jnp.where(proj > 0, proj, jnp.exp(jnp.minimum(proj, 0.0)) - 1.0) + 1.0
            if unit < GROUPS:
                feat = jnp.where(first, proj, feat)
            out_ref[:, unit * LANES : (unit + 1) * LANES] = feat.astype(jnp.bfloat16)


def project(tokens, weights):
    rows, depth = tokens.shape
    steps = 4
    return pl.pallas_call(
        project_kernel,
        out_shape=jax.ShapeDtypeStruct((rows, steps * BLOCK), jnp.bfloat16),
        compiler_params=PARAMS,
        cost_estimate=cost(2 * rows * depth * steps * BLOCK, 4 * 1024 * 1024),
        name="project",
    )(tokens, weights)


def unit_of(core, mine_ref, theirs_ref, unit):
    at = slice(unit * LANES, (unit + 1) * LANES)
    return jnp.where(lax.axis_index("core") == core, mine_ref[:, at], theirs_ref[:, at])


def state_kernel(mine_ref, theirs_ref, values_ref, tiles_ref):
    lane = lax.broadcasted_iota(jnp.int32, (HEAD_WIDTH, LANES), 1) // HEAD_WIDTH
    tiles_ref[...] = jnp.zeros_like(tiles_ref)
    for g in range(GROUPS):
        values = unit_of(0, mine_ref, theirs_ref, g)
        kfeat = unit_of(1, mine_ref, theirs_ref, 2 + g)
        values_ref[:, g * LANES : (g + 1) * LANES] = values
        square = lax.dot_general(
            kfeat, values, (((0,), (0,)), ((), ())), preferred_element_type=jnp.float32
        )
        packed = jnp.zeros((HEAD_WIDTH, LANES), jnp.float32)
        for h in range(LANES // HEAD_WIDTH):
            packed = jnp.where(lane == h, square[h * HEAD_WIDTH : (h + 1) * HEAD_WIDTH], packed)
        for t in range(4):
            tiles_ref[4 * g + t] = packed[8 * t : 8 * t + 8]
        tiles_ref[4 * GROUPS, g : g + 1, :] = jnp.sum(
            kfeat.astype(jnp.float32), axis=0, keepdims=True
        )


def states(mine, theirs):
    rows = mine.shape[0]
    return pl.pallas_call(
        state_kernel,
        out_shape=(
            jax.ShapeDtypeStruct((rows, GROUPS * LANES), jnp.bfloat16),
            jax.ShapeDtypeStruct((TILES, 8, LANES), jnp.float32),
        ),
        compiler_params=PARAMS,
        cost_estimate=cost(2 * rows * GROUPS * LANES * LANES, 2 * 1024 * 1024),
        name="states",
    )(mine, theirs)


def conv_kernel(before_ref, values_ref, after_ref, weight_ref, out_ref):
    zeros = jnp.zeros((FW, LANES), jnp.float32)
    rows = FH * FW
    x = lax.broadcasted_iota(jnp.int32, (rows, LANES), 0) % FW
    weight = weight_ref[...].astype(jnp.float32)
    frames = [
        jnp.concatenate([zeros, ref[...].astype(jnp.float32), zeros], axis=0)
        for ref in (before_ref, values_ref, after_ref)
    ]
    sums = []
    for c in range(3):
        total = None
        for a in range(3):
            for b in range(3):
                tap = 9 * a + 3 * b + c
                term = frames[a][b * FW : b * FW + rows] * weight[tap : tap + 1]
                total = term if total is None else total + term
        sums.append(total)
    left = jnp.where(x == 0, 0.0, pltpu.roll(sums[0], 1, 0))
    right = jnp.where(x == FW - 1, 0.0, pltpu.roll(sums[2], rows - 1, 0))
    out_ref[...] = left + sums[1] + right


def convolve(before, values, after, weight):
    rows, width = values.shape
    block = pl.BlockSpec((rows, LANES), lambda i: (0, i))
    return pl.pallas_call(
        conv_kernel,
        grid=(width // LANES,),
        in_specs=[block, block, block, pl.BlockSpec((27, LANES), lambda i: (0, i))],
        out_specs=block,
        out_shape=jax.ShapeDtypeStruct((rows, width), jnp.float32),
        compiler_params=PARAMS,
        cost_estimate=cost(54 * rows * width, 2 * 1024 * 1024),
        name="convolve",
    )(before, values, after, weight)


def split_dot(a, b):
    high = b.astype(jnp.bfloat16)
    low = (b - high.astype(jnp.float32)).astype(jnp.bfloat16)
    return jnp.dot(
        jnp.concatenate([a, a], axis=1),
        jnp.concatenate([high, low], axis=0),
        preferred_element_type=jnp.float32,
    )


def attend_kernel(mine_ref, theirs_ref, tiles_ref, local_ref, out_ref):
    row = lax.broadcasted_iota(jnp.int32, (LANES, LANES), 0) // HEAD_WIDTH
    lane = lax.broadcasted_iota(jnp.int32, (LANES, LANES), 1) // HEAD_WIDTH
    same = row == lane
    for g in range(GROUPS):
        core, unit = (0, GROUPS + g) if g < 3 else (1, g - 3)
        qfeat = unit_of(core, mine_ref, theirs_ref, unit)
        packed = tiles_ref[4 * g : 4 * g + 4].reshape(HEAD_WIDTH, LANES)
        state = jnp.where(same, jnp.concatenate([packed] * 4, axis=0), 0.0)
        ksum = jnp.broadcast_to(tiles_ref[4 * GROUPS, g : g + 1, :], (LANES, LANES)).T
        ksum = jnp.where(same, ksum, 0.0)
        both = split_dot(qfeat, jnp.concatenate([state, ksum], axis=1))
        cols = slice(g * LANES, (g + 1) * LANES)
        out_ref[:, cols] = both[:, :LANES] / both[:, LANES:] + local_ref[:, cols]


def attend(mine, theirs, tiles, local):
    rows, width = local.shape
    return pl.pallas_call(
        attend_kernel,
        out_shape=jax.ShapeDtypeStruct((rows, width), jnp.float32),
        compiler_params=PARAMS,
        cost_estimate=cost(8 * rows * width * LANES, 3 * 1024 * 1024),
        name="attend",
    )(mine, theirs, tiles, local)


def spread_crossed(block, turn):
    ys, xs = lax.axis_size("y"), lax.axis_size("x")
    place = lambda core, y, x: (core * ys + y) * xs + x
    along_x = [[place(turn, y, x) for x in range(xs)] for y in range(ys)]
    along_y = [[place(1 - turn, y, x) for y in range(ys)] for x in range(xs)]
    blocks = jnp.broadcast_to(block[None], (xs,) + block.shape)
    return lax.all_to_all(
        blocks, ("core", "y", "x"), 0, 0, tiled=True, axis_index_groups=along_x + along_y
    )


def swap(block):
    return lax.ppermute(block, "core", [(0, 1), (1, 0)])


def pick(w_query, w_key, w_value):
    pad = jnp.zeros((w_query.shape[0], LANES), w_query.dtype)
    cat = jnp.concatenate([w_value, w_query, w_key, pad], axis=1)
    place = 4 * lax.axis_index("core") + lax.axis_index("y")
    mine = lax.dynamic_slice_in_dim(cat, place * BLOCK, BLOCK, axis=1)
    return jnp.concatenate([mine[:, :LANES], mine[:, LANES:]], axis=0)


def body(tokens, gain, w_query, w_key, w_value, conv_weight):
    rows = w_query.shape[0]
    normed = norm(tokens, gain)
    other = swap(normed)
    column = spread(pick(w_query, w_key, w_value), ZAX)
    column = jnp.concatenate([column[:, :rows], column[:, rows:]], axis=2).reshape(-1, BLOCK)
    column, other = lax.optimization_barrier((column, other))
    weights = spread_crossed(spread_crossed(column, 0).reshape(-1, BLOCK), 1)
    weights = weights.reshape((-1,) + column.shape)

    theirs = swap(project(other, weights))
    mine = project(normed, weights)
    values, tiles = states(mine, theirs)
    count = lax.axis_size(TM)
    before = lax.ppermute(values, TM, [(i, i + 1) for i in range(count - 1)])
    after = lax.ppermute(values, TM, [(i + 1, i) for i in range(count - 1)])

    share = TILES // lax.axis_size(NEAR)
    part = jnp.sum(exchange(tiles, NEAR).reshape((-1, share) + tiles.shape[1:]), axis=0)
    part = part.astype(jnp.bfloat16).reshape(-1, LANES)
    part = spread(part, ZAX).astype(jnp.float32)
    part = jnp.sum(part.reshape((lax.axis_size("zh"), -1) + part.shape[1:]), axis=0)
    local = convolve(before, values, after, conv_weight)
    tiles = spread(part.reshape((-1,) + tiles.shape[1:]), "x").reshape(tiles.shape)
    return attend(mine, theirs, tiles, local)


def solution(mesh):
    fine = Mesh(mesh.devices.reshape(4, 2, 4, 8, 2), AXES)
    rows = P(AXES, None)
    split = P(TM, None)
    return jax.shard_map(
        body, mesh=fine, in_specs=(rows, P(), split, split, split, P()), out_specs=rows, check_vma=False
    )
```

```python
import jax
import jax.numpy as jnp
from jax import lax
from jax.experimental import pallas as pl
from jax.experimental.pallas import tpu as pltpu
from jax.sharding import Mesh
from jax.sharding import PartitionSpec as P

HEAD_WIDTH = 32
FH = 8
FW = 32
LANES = 128
BLOCK = 2 * LANES
GROUPS = 5
TILES = 24

AXES = ("y", "core", "x", "zh", "zl")
ZAX = ("zh", "zl")
TM = ("x", "zh", "zl")
NEAR = ("x", "zl")
PARAMS = pltpu.CompilerParams(vmem_limit_bytes=12 * 1024 * 1024)


def cost(flops, nbytes):
    return pl.CostEstimate(flops=flops, bytes_accessed=nbytes, transcendentals=0)


def exchange(blocks, axes):
    return lax.all_to_all(blocks, axes, 0, 0, tiled=True)


def spread(block, axes):
    count = lax.axis_size(axes)
    return exchange(jnp.broadcast_to(block[None], (count,) + block.shape), axes)


def norm_kernel(tokens_ref, gain_ref, out_ref):
    x = tokens_ref[...].astype(jnp.float32)
    scale = lax.rsqrt(jnp.mean(x * x, axis=1, keepdims=True) + 1e-06)
    out_ref[...] = (x * scale * gain_ref[...].astype(jnp.float32)[None]).astype(jnp.bfloat16)


def norm(tokens, gain):
    return pl.pallas_call(
        norm_kernel,
        out_shape=jax.ShapeDtypeStruct(tokens.shape, jnp.bfloat16),
        compiler_params=PARAMS,
        cost_estimate=cost(10 * tokens.size, 4 * tokens.size),
        name="norm",
    )(tokens, gain)


def project_kernel(tokens_ref, weight_ref, out_ref):
    first = lax.axis_index("core") == 0
    for step in range(4):
        places = [jnp.where(first, 4 * step + x, 4 * x + step) for x in range(4)]
        weight = jnp.concatenate([weight_ref[place] for place in places], axis=0)
        both = jnp.dot(tokens_ref[...], weight, preferred_element_type=jnp.float32)
        for half in range(2):
            unit = 2 * step + half
            proj = both[:, half * LANES : (half + 1) * LANES]
            feat = jnp.where(proj > 0, proj, jnp.exp(jnp.minimum(proj, 0.0)) - 1.0) + 1.0
            if unit < GROUPS:
                feat = jnp.where(first, proj, feat)
            out_ref[:, unit * LANES : (unit + 1) * LANES] = feat.astype(jnp.bfloat16)


def project(tokens, weights):
    rows, depth = tokens.shape
    steps = 4
    return pl.pallas_call(
        project_kernel,
        out_shape=jax.ShapeDtypeStruct((rows, steps * BLOCK), jnp.bfloat16),
        compiler_params=PARAMS,
        cost_estimate=cost(2 * rows * depth * steps * BLOCK, 4 * 1024 * 1024),
        name="project",
    )(tokens, weights)


def unit_of(core, mine_ref, theirs_ref, unit):
    at = slice(unit * LANES, (unit + 1) * LANES)
    return jnp.where(lax.axis_index("core") == core, mine_ref[:, at], theirs_ref[:, at])


def state_kernel(mine_ref, theirs_ref, values_ref, tiles_ref):
    lane = lax.broadcasted_iota(jnp.int32, (HEAD_WIDTH, LANES), 1) // HEAD_WIDTH
    tiles_ref[...] = jnp.zeros_like(tiles_ref)
    for g in range(GROUPS):
        values = unit_of(0, mine_ref, theirs_ref, g)
        kfeat = unit_of(1, mine_ref, theirs_ref, 2 + g)
        values_ref[:, g * LANES : (g + 1) * LANES] = values
        square = lax.dot_general(
            kfeat, values, (((0,), (0,)), ((), ())), preferred_element_type=jnp.float32
        )
        packed = jnp.zeros((HEAD_WIDTH, LANES), jnp.float32)
        for h in range(LANES // HEAD_WIDTH):
            packed = jnp.where(lane == h, square[h * HEAD_WIDTH : (h + 1) * HEAD_WIDTH], packed)
        for t in range(4):
            tiles_ref[4 * g + t] = packed[8 * t : 8 * t + 8]
        tiles_ref[4 * GROUPS, g : g + 1, :] = jnp.sum(
            kfeat.astype(jnp.float32), axis=0, keepdims=True
        )


def states(mine, theirs):
    rows = mine.shape[0]
    return pl.pallas_call(
        state_kernel,
        out_shape=(
            jax.ShapeDtypeStruct((rows, GROUPS * LANES), jnp.bfloat16),
            jax.ShapeDtypeStruct((TILES, 8, LANES), jnp.float32),
        ),
        compiler_params=PARAMS,
        cost_estimate=cost(2 * rows * GROUPS * LANES * LANES, 2 * 1024 * 1024),
        name="states",
    )(mine, theirs)


def query_kernel(mine_ref, theirs_ref, out_ref):
    for g in range(GROUPS):
        core, unit = (0, GROUPS + g) if g < 3 else (1, g - 3)
        out_ref[:, g * LANES : (g + 1) * LANES] = unit_of(core, mine_ref, theirs_ref, unit)


def queries(mine, theirs):
    rows = mine.shape[0]
    return pl.pallas_call(
        query_kernel,
        out_shape=jax.ShapeDtypeStruct((rows, GROUPS * LANES), jnp.bfloat16),
        compiler_params=PARAMS,
        cost_estimate=cost(rows * GROUPS * LANES, 2 * 1024 * 1024),
        name="queries",
    )(mine, theirs)


def conv_kernel(before_ref, values_ref, after_ref, weight_ref, out_ref):
    zeros = jnp.zeros((FW, LANES), jnp.float32)
    rows = FH * FW
    x = lax.broadcasted_iota(jnp.int32, (rows, LANES), 0) % FW
    weight = weight_ref[...].astype(jnp.float32)
    frames = [
        jnp.concatenate([zeros, ref[...].astype(jnp.float32), zeros], axis=0)
        for ref in (before_ref, values_ref, after_ref)
    ]
    sums = []
    for c in range(3):
        total = None
        for a in range(3):
            for b in range(3):
                tap = 9 * a + 3 * b + c
                term = frames[a][b * FW : b * FW + rows] * weight[tap : tap + 1]
                total = term if total is None else total + term
        sums.append(total)
    left = jnp.where(x == 0, 0.0, pltpu.roll(sums[0], 1, 0))
    right = jnp.where(x == FW - 1, 0.0, pltpu.roll(sums[2], rows - 1, 0))
    out_ref[...] = left + sums[1] + right


def convolve(before, values, after, weight):
    rows, width = values.shape
    block = pl.BlockSpec((rows, LANES), lambda i: (0, i))
    return pl.pallas_call(
        conv_kernel,
        grid=(width // LANES,),
        in_specs=[block, block, block, pl.BlockSpec((27, LANES), lambda i: (0, i))],
        out_specs=block,
        out_shape=jax.ShapeDtypeStruct((rows, width), jnp.float32),
        compiler_params=PARAMS,
        cost_estimate=cost(54 * rows * width, 2 * 1024 * 1024),
        name="convolve",
    )(before, values, after, weight)


def split_dot(a, b):
    high = b.astype(jnp.bfloat16)
    low = (b - high.astype(jnp.float32)).astype(jnp.bfloat16)
    return jnp.dot(
        jnp.concatenate([a, a], axis=1),
        jnp.concatenate([high, low], axis=0),
        preferred_element_type=jnp.float32,
    )


def attend_kernel(query_ref, tiles_ref, local_ref, out_ref):
    row = lax.broadcasted_iota(jnp.int32, (LANES, LANES), 0) // HEAD_WIDTH
    lane = lax.broadcasted_iota(jnp.int32, (LANES, LANES), 1) // HEAD_WIDTH
    same = row == lane
    for g in range(GROUPS):
        qfeat = query_ref[:, g * LANES : (g + 1) * LANES]
        packed = tiles_ref[4 * g : 4 * g + 4].reshape(HEAD_WIDTH, LANES)
        state = jnp.where(same, jnp.concatenate([packed] * 4, axis=0), 0.0)
        ksum = jnp.broadcast_to(tiles_ref[4 * GROUPS, g : g + 1, :], (LANES, LANES)).T
        ksum = jnp.where(same, ksum, 0.0)
        both = split_dot(qfeat, jnp.concatenate([state, ksum], axis=1))
        cols = slice(g * LANES, (g + 1) * LANES)
        out_ref[:, cols] = both[:, :LANES] / both[:, LANES:] + local_ref[:, cols]


def attend(query, tiles, local):
    rows, width = local.shape
    return pl.pallas_call(
        attend_kernel,
        out_shape=jax.ShapeDtypeStruct((rows, width), jnp.float32),
        compiler_params=PARAMS,
        cost_estimate=cost(8 * rows * width * LANES, 3 * 1024 * 1024),
        name="attend",
    )(query, tiles, local)


def spread_crossed(block, turn):
    ys, xs = lax.axis_size("y"), lax.axis_size("x")
    place = lambda core, y, x: (core * ys + y) * xs + x
    along_x = [[place(turn, y, x) for x in range(xs)] for y in range(ys)]
    along_y = [[place(1 - turn, y, x) for y in range(ys)] for x in range(xs)]
    blocks = jnp.broadcast_to(block[None], (xs,) + block.shape)
    return lax.all_to_all(
        blocks, ("core", "y", "x"), 0, 0, tiled=True, axis_index_groups=along_x + along_y
    )


def swap(block):
    return lax.ppermute(block, "core", [(0, 1), (1, 0)])


def pick(w_query, w_key, w_value):
    pad = jnp.zeros((w_query.shape[0], LANES), w_query.dtype)
    cat = jnp.concatenate([w_value, w_query, w_key, pad], axis=1)
    place = 4 * lax.axis_index("core") + lax.axis_index("y")
    mine = lax.dynamic_slice_in_dim(cat, place * BLOCK, BLOCK, axis=1)
    return jnp.concatenate([mine[:, :LANES], mine[:, LANES:]], axis=0)


def body(tokens, gain, w_query, w_key, w_value, conv_weight):
    rows = w_query.shape[0]
    normed = norm(tokens, gain)
    other = swap(normed)
    column = spread(pick(w_query, w_key, w_value), ZAX)
    column = jnp.concatenate([column[:, :rows], column[:, rows:]], axis=2).reshape(-1, BLOCK)
    column, other = lax.optimization_barrier((column, other))
    weights = spread_crossed(spread_crossed(column, 0).reshape(-1, BLOCK), 1)
    weights = weights.reshape((-1,) + column.shape)

    theirs = swap(project(other, weights))
    mine = project(normed, weights)
    values, tiles = states(mine, theirs)
    count = lax.axis_size(TM)
    before = lax.ppermute(values, TM, [(i, i + 1) for i in range(count - 1)])
    after = lax.ppermute(values, TM, [(i + 1, i) for i in range(count - 1)])

    share = TILES // lax.axis_size(NEAR)
    part = jnp.sum(exchange(tiles, NEAR).reshape((-1, share) + tiles.shape[1:]), axis=0)
    part = part.astype(jnp.bfloat16).reshape(-1, LANES)
    part = spread(part, ZAX).astype(jnp.float32)
    part = jnp.sum(part.reshape((lax.axis_size("zh"), -1) + part.shape[1:]), axis=0)
    local = convolve(before, values, after, conv_weight)
    tiles = spread(part.reshape((-1,) + tiles.shape[1:]), "x").reshape(tiles.shape)
    return attend(queries(mine, theirs), tiles, local)


def solution(mesh):
    fine = Mesh(mesh.devices.reshape(4, 2, 4, 8, 2), AXES)
    rows = P(AXES, None)
    split = P(TM, None)
    return jax.shard_map(
        body, mesh=fine, in_specs=(rows, P(), split, split, split, P()), out_specs=rows, check_vma=False
    )
```

```python
import jax
import jax.numpy as jnp
from jax import lax
from jax.experimental import pallas as pl
from jax.experimental.pallas import tpu as pltpu
from jax.sharding import Mesh
from jax.sharding import PartitionSpec as P

HEAD_WIDTH = 32
FH = 8
FW = 32
LANES = 128
BLOCK = 2 * LANES
GROUPS = 5
TILES = 24

AXES = ("y", "core", "x", "zh", "zl")
ZAX = ("zh", "zl")
TM = ("x", "zh", "zl")
NEAR = ("x", "zl")
PARAMS = pltpu.CompilerParams(vmem_limit_bytes=12 * 1024 * 1024)


def cost(flops, nbytes):
    return pl.CostEstimate(flops=flops, bytes_accessed=nbytes, transcendentals=0)


def exchange(blocks, axes):
    return lax.all_to_all(blocks, axes, 0, 0, tiled=True)


def spread(block, axes):
    count = lax.axis_size(axes)
    return exchange(jnp.broadcast_to(block[None], (count,) + block.shape), axes)


def norm_kernel(tokens_ref, gain_ref, out_ref):
    x = tokens_ref[...].astype(jnp.float32)
    scale = lax.rsqrt(jnp.mean(x * x, axis=1, keepdims=True) + 1e-06)
    out_ref[...] = (x * scale * gain_ref[...].astype(jnp.float32)[None]).astype(jnp.bfloat16)


def norm(tokens, gain):
    return pl.pallas_call(
        norm_kernel,
        out_shape=jax.ShapeDtypeStruct(tokens.shape, jnp.bfloat16),
        compiler_params=PARAMS,
        cost_estimate=cost(10 * tokens.size, 4 * tokens.size),
        name="norm",
    )(tokens, gain)


def project_kernel(tokens_ref, weight_ref, out_ref):
    first = lax.axis_index("core") == 0
    for step in range(4):
        places = [jnp.where(first, 4 * step + x, 4 * x + step) for x in range(4)]
        weight = jnp.concatenate([weight_ref[place] for place in places], axis=0)
        both = jnp.dot(tokens_ref[...], weight, preferred_element_type=jnp.float32)
        for half in range(2):
            unit = 2 * step + half
            proj = both[:, half * LANES : (half + 1) * LANES]
            feat = jnp.where(proj > 0, proj + 1.0, jnp.exp(jnp.minimum(proj, 0.0)))
            if unit < GROUPS:
                feat = jnp.where(first, proj, feat)
            out_ref[:, unit * LANES : (unit + 1) * LANES] = feat.astype(jnp.bfloat16)


def project(tokens, weights):
    rows, depth = tokens.shape
    steps = 4
    return pl.pallas_call(
        project_kernel,
        out_shape=jax.ShapeDtypeStruct((rows, steps * BLOCK), jnp.bfloat16),
        compiler_params=PARAMS,
        cost_estimate=cost(2 * rows * depth * steps * BLOCK, 4 * 1024 * 1024),
        name="project",
    )(tokens, weights)


def unit_of(core, mine_ref, theirs_ref, unit):
    at = slice(unit * LANES, (unit + 1) * LANES)
    return jnp.where(lax.axis_index("core") == core, mine_ref[:, at], theirs_ref[:, at])


def state_kernel(mine_ref, theirs_ref, values_ref, tiles_ref):
    lane = lax.broadcasted_iota(jnp.int32, (HEAD_WIDTH, LANES), 1) // HEAD_WIDTH
    tiles_ref[...] = jnp.zeros_like(tiles_ref)
    for g in range(GROUPS):
        values = unit_of(0, mine_ref, theirs_ref, g)
        kfeat = unit_of(1, mine_ref, theirs_ref, 2 + g)
        values_ref[:, g * LANES : (g + 1) * LANES] = values
        square = lax.dot_general(
            kfeat, values, (((0,), (0,)), ((), ())), preferred_element_type=jnp.float32
        )
        packed = jnp.zeros((HEAD_WIDTH, LANES), jnp.float32)
        for h in range(LANES // HEAD_WIDTH):
            packed = jnp.where(lane == h, square[h * HEAD_WIDTH : (h + 1) * HEAD_WIDTH], packed)
        for t in range(4):
            tiles_ref[4 * g + t] = packed[8 * t : 8 * t + 8]
        tiles_ref[4 * GROUPS, g : g + 1, :] = jnp.sum(
            kfeat.astype(jnp.float32), axis=0, keepdims=True
        )


def states(mine, theirs):
    rows = mine.shape[0]
    return pl.pallas_call(
        state_kernel,
        out_shape=(
            jax.ShapeDtypeStruct((rows, GROUPS * LANES), jnp.bfloat16),
            jax.ShapeDtypeStruct((TILES, 8, LANES), jnp.float32),
        ),
        compiler_params=PARAMS,
        cost_estimate=cost(2 * rows * GROUPS * LANES * LANES, 2 * 1024 * 1024),
        name="states",
    )(mine, theirs)


def query_kernel(mine_ref, theirs_ref, out_ref):
    for g in range(GROUPS):
        core, unit = (0, GROUPS + g) if g < 3 else (1, g - 3)
        out_ref[:, g * LANES : (g + 1) * LANES] = unit_of(core, mine_ref, theirs_ref, unit)


def queries(mine, theirs):
    rows = mine.shape[0]
    return pl.pallas_call(
        query_kernel,
        out_shape=jax.ShapeDtypeStruct((rows, GROUPS * LANES), jnp.bfloat16),
        compiler_params=PARAMS,
        cost_estimate=cost(rows * GROUPS * LANES, 2 * 1024 * 1024),
        name="queries",
    )(mine, theirs)


def conv_kernel(before_ref, values_ref, after_ref, weight_ref, out_ref):
    zeros = jnp.zeros((FW, LANES), jnp.float32)
    rows = FH * FW
    x = lax.broadcasted_iota(jnp.int32, (rows, LANES), 0) % FW
    weight = weight_ref[...].astype(jnp.float32)
    frames = [
        jnp.concatenate([zeros, ref[...].astype(jnp.float32), zeros], axis=0)
        for ref in (before_ref, values_ref, after_ref)
    ]
    sums = []
    for c in range(3):
        total = None
        for a in range(3):
            for b in range(3):
                tap = 9 * a + 3 * b + c
                term = frames[a][b * FW : b * FW + rows] * weight[tap : tap + 1]
                total = term if total is None else total + term
        sums.append(total)
    left = jnp.where(x == 0, 0.0, pltpu.roll(sums[0], 1, 0))
    right = jnp.where(x == FW - 1, 0.0, pltpu.roll(sums[2], rows - 1, 0))
    out_ref[...] = left + sums[1] + right


def convolve(before, values, after, weight):
    rows, width = values.shape
    block = pl.BlockSpec((rows, LANES), lambda i: (0, i))
    return pl.pallas_call(
        conv_kernel,
        grid=(width // LANES,),
        in_specs=[block, block, block, pl.BlockSpec((27, LANES), lambda i: (0, i))],
        out_specs=block,
        out_shape=jax.ShapeDtypeStruct((rows, width), jnp.float32),
        compiler_params=PARAMS,
        cost_estimate=cost(54 * rows * width, 2 * 1024 * 1024),
        name="convolve",
    )(before, values, after, weight)


def split_dot(a, b):
    high = b.astype(jnp.bfloat16)
    low = (b - high.astype(jnp.float32)).astype(jnp.bfloat16)
    return jnp.dot(
        jnp.concatenate([a, a], axis=1),
        jnp.concatenate([high, low], axis=0),
        preferred_element_type=jnp.float32,
    )


def attend_kernel(query_ref, tiles_ref, local_ref, out_ref):
    row = lax.broadcasted_iota(jnp.int32, (LANES, LANES), 0) // HEAD_WIDTH
    lane = lax.broadcasted_iota(jnp.int32, (LANES, LANES), 1) // HEAD_WIDTH
    same = row == lane
    for g in range(GROUPS):
        qfeat = query_ref[:, g * LANES : (g + 1) * LANES]
        packed = tiles_ref[4 * g : 4 * g + 4].reshape(HEAD_WIDTH, LANES)
        state = jnp.where(same, jnp.concatenate([packed] * 4, axis=0), 0.0)
        ksum = jnp.broadcast_to(tiles_ref[4 * GROUPS, g : g + 1, :], (LANES, LANES)).T
        ksum = jnp.where(same, ksum, 0.0)
        both = split_dot(qfeat, jnp.concatenate([state, ksum], axis=1))
        cols = slice(g * LANES, (g + 1) * LANES)
        out_ref[:, cols] = both[:, :LANES] / both[:, LANES:] + local_ref[:, cols]


def attend(query, tiles, local):
    rows, width = local.shape
    return pl.pallas_call(
        attend_kernel,
        out_shape=jax.ShapeDtypeStruct((rows, width), jnp.float32),
        compiler_params=PARAMS,
        cost_estimate=cost(8 * rows * width * LANES, 3 * 1024 * 1024),
        name="attend",
    )(query, tiles, local)


def spread_crossed(block, turn):
    ys, xs = lax.axis_size("y"), lax.axis_size("x")
    place = lambda core, y, x: (core * ys + y) * xs + x
    along_x = [[place(turn, y, x) for x in range(xs)] for y in range(ys)]
    along_y = [[place(1 - turn, y, x) for y in range(ys)] for x in range(xs)]
    blocks = jnp.broadcast_to(block[None], (xs,) + block.shape)
    return lax.all_to_all(
        blocks, ("core", "y", "x"), 0, 0, tiled=True, axis_index_groups=along_x + along_y
    )


def swap(block):
    return lax.ppermute(block, "core", [(0, 1), (1, 0)])


def pick(w_query, w_key, w_value):
    pad = jnp.zeros((w_query.shape[0], LANES), w_query.dtype)
    cat = jnp.concatenate([w_value, w_query, w_key, pad], axis=1)
    place = 4 * lax.axis_index("core") + lax.axis_index("y")
    mine = lax.dynamic_slice_in_dim(cat, place * BLOCK, BLOCK, axis=1)
    return jnp.concatenate([mine[:, :LANES], mine[:, LANES:]], axis=0)


def body(tokens, gain, w_query, w_key, w_value, conv_weight):
    rows = w_query.shape[0]
    normed = norm(tokens, gain)
    other = swap(normed)
    column = spread(pick(w_query, w_key, w_value), ZAX)
    column = jnp.concatenate([column[:, :rows], column[:, rows:]], axis=2).reshape(-1, BLOCK)
    column, other = lax.optimization_barrier((column, other))
    weights = spread_crossed(spread_crossed(column, 0).reshape(-1, BLOCK), 1)
    weights = weights.reshape((-1,) + column.shape)

    theirs = swap(project(other, weights))
    mine = project(normed, weights)
    values, tiles = states(mine, theirs)
    count = lax.axis_size(TM)
    before = lax.ppermute(values, TM, [(i, i + 1) for i in range(count - 1)])
    after = lax.ppermute(values, TM, [(i + 1, i) for i in range(count - 1)])

    share = TILES // lax.axis_size(NEAR)
    part = jnp.sum(exchange(tiles, NEAR).reshape((-1, share) + tiles.shape[1:]), axis=0)
    part = part.astype(jnp.bfloat16).reshape(-1, LANES)
    part = spread(part, ZAX).astype(jnp.float32)
    part = jnp.sum(part.reshape((lax.axis_size("zh"), -1) + part.shape[1:]), axis=0)
    local = convolve(before, values, after, conv_weight)
    tiles = spread(part.reshape((-1,) + tiles.shape[1:]), "x").reshape(tiles.shape)
    return attend(queries(mine, theirs), tiles, local)


def solution(mesh):
    fine = Mesh(mesh.devices.reshape(4, 2, 4, 8, 2), AXES)
    rows = P(AXES, None)
    split = P(TM, None)
    return jax.shard_map(
        body, mesh=fine, in_specs=(rows, P(), split, split, split, P()), out_specs=rows, check_vma=False
    )
```
